256 devices in a mesh: tm: 16 (over y, z_lo), row: 4 (over x), col: 4 (over z_hi, core).
Axes of the slice: x: 4, y: 4, z: 8 (z_hi: 2, z_lo: 4; z = z_hi * 4 + z_lo), core: 2. Of those that a mesh axis runs over, the one named last changes fastest.
Arguments:
- frame_features: bfloat16 [64, 16, 512, 128], P('tm', 'row', 'col'), may hold values from -6 to 6
- key_features: bfloat16 [16, 16, 512, 128], P('tm', 'row', 'col'), may hold values from -6 to 6
- key_index: int32 [64, 1], P('tm'), may hold values from 0 to 15, as said below
- motion_weight: bfloat16 [81, 128], replicated, may hold values from -0.625 to 0.625
- joint_weight: bfloat16 [3, 3, 256, 128], replicated, may hold values from -0.125 to 0.125
- dilated_weight: bfloat16 [3, 3, 128, 128], replicated, may hold values from -0.1875 to 0.1875
- flow_weight: bfloat16 [2, 3, 3, 128], replicated, may hold values from -0.1875 to 0.1875
Outputs:
- flow_update: float32 [64, 2, 16, 512], P('tm', None, 'row', 'col')
The draws below stay inside these ranges and needn't reach their ends.
Inputs may be any that keep to these rules, and one draw needn't show every extreme that they name: `key_index`: frames come in blocks of 4 in order, block b holding frames b * 4 to (b + 1) * 4 - 1; a frame of block b names group b or group b - 1 (block 0 names only group 0); within a block the frames that name b - 1 come first; in every block b of 1 or more the first frame names b - 1, and the last frame of every block names b.
All inputs are finite; a program needn't handle non-finite values.
Results may differ from the reference program's by a relative error of at most 0.0048.
Values may be sent and summed in bfloat16 or wider, within the bound.
A program may use at most 64 MiB of HBM per device.

```python
import math
import jax
import jax.numpy as jnp
from jax import lax

C = 128
RAD = 4
FR_DEV = 4
DISP = 81
GROUPS = 16
FRAMES = 64
H = 16
W = 512


def draw_key_index(key, part):
    starts = jax.random.randint(jax.random.fold_in(key, 17), (GROUPS,), 1, 4, dtype=jnp.int32)
    frame_ids = jnp.arange(FRAMES, dtype=jnp.int32)
    blocks = frame_ids // FR_DEV
    within = frame_ids % FR_DEV
    earlier = (within < starts[blocks]).astype(jnp.int32)
    groups = jnp.maximum(blocks - earlier, 0)
    return groups.reshape(FRAMES, 1).astype(jnp.int32)


def shard_levels(own_key, dims, shards, least, top_value):
    def one(axis_at, shards_of):
        draws = jax.random.uniform(jax.random.fold_in(jax.random.fold_in(own_key, 6), axis_at), (shards_of,), jnp.float32, least / len(shards), top_value / len(shards))
        return jnp.repeat(jnp.exp(draws), dims[axis_at] // shards_of).reshape((-1,) + (1,) * (len(dims) - axis_at - 1))

    factor_of = one(*shards[0])
    for cut in shards[1:]:
        factor_of = factor_of * one(*cut)
    return factor_of


def noise(key, extent, scale, most, split=(), held_as=jnp.bfloat16):
    entries = jax.random.normal(key, extent, jnp.float32) * scale
    if len(split) > 0:
        entries = shard_levels(key, extent, split, -0.22, 0.18) * entries
    return jnp.clip(entries, min=-most, max=most).astype(held_as)


def setup_inputs(seed: int = 0) -> dict:
    splits = jax.random.split(jax.random.key(seed), 8)
    frame_features = noise(splits[0], (FRAMES, H, W, C), 1.0, 6.0, ((0, 16), (1, 4), (2, 4)))
    key_features = noise(splits[1], (GROUPS, H, W, C), 1.0, 6.0, ((0, 16), (1, 4), (2, 4)))
    key_index = draw_key_index(jax.random.fold_in(splits[7], 71), 0)
    motion_weight = noise(splits[3], (DISP, C), DISP ** -0.5, 0.625)
    joint_weight = noise(splits[4], (3, 3, 2 * C, C), (9 * 2 * C) ** -0.5, 0.125)
    dilated_weight = noise(splits[5], (3, 3, C, C), (9 * C) ** -0.5, 0.1875)
    flow_weight = noise(splits[6], (2, 3, 3, C), (9 * C) ** -0.5, 0.1875)
    return dict(frame_features=frame_features, key_features=key_features, key_index=key_index, motion_weight=motion_weight, joint_weight=joint_weight, dilated_weight=dilated_weight, flow_weight=flow_weight)


def convolve(padded, weight, spread, height, width):
    totals = jnp.zeros((height * width, weight.shape[3]), jnp.float32)
    for tap_row in range(3):
        for tap_column in range(3):
            window = padded[tap_row * spread:tap_row * spread + height, tap_column * spread:tap_column * spread + width, :]
            totals = totals + jnp.dot(window.reshape(height * width, window.shape[2]), weight[tap_row, tap_column], preferred_element_type=jnp.float32)
    return totals.reshape(height, width, weight.shape[3])

def reference(frame_features, key_features, key_index, motion_weight, joint_weight, dilated_weight, flow_weight):
    height = frame_features.shape[1]
    width = frame_features.shape[2]
    window_size = 2 * RAD + 1
    scaling = 1.0 / math.sqrt(C)
    flow_taps = jnp.transpose(flow_weight, (1, 2, 3, 0))

    def one_frame(inputs):
        frame, group = inputs
        keyframe = lax.dynamic_index_in_dim(key_features, group, 0, keepdims=False)
        queries = frame.astype(jnp.float32)
        padded_key = jnp.pad(keyframe.astype(jnp.float32), ((RAD, RAD), (RAD, RAD), (0, 0)))
        columns = []
        for shift_row in range(window_size):
            for shift_column in range(window_size):
                window = padded_key[shift_row:shift_row + height, shift_column:shift_column + width, :]
                columns.append(lax.optimization_barrier(jnp.sum(queries * window, axis=-1)))
        correlation = (jnp.stack(columns, axis=-1) * scaling).astype(jnp.bfloat16)
        motion = jax.nn.relu(jnp.dot(correlation.reshape(height * width, window_size * window_size), motion_weight, preferred_element_type=jnp.float32))
        motion = motion.astype(jnp.bfloat16).reshape(height, width, motion_weight.shape[1])
        joined = jnp.concatenate([motion, frame], axis=-1)
        hidden_one = jax.nn.relu(convolve(jnp.pad(joined, ((1, 1), (1, 1), (0, 0))), joint_weight, 1, height, width)).astype(jnp.bfloat16)
        hidden_two = jax.nn.relu(convolve(jnp.pad(hidden_one, ((2, 2), (2, 2), (0, 0))), dilated_weight, 2, height, width)).astype(jnp.bfloat16)
        flow = convolve(jnp.pad(hidden_two, ((1, 1), (1, 1), (0, 0))), flow_taps, 1, height, width)
        return jnp.transpose(flow, (2, 0, 1))
    return lax.map(one_frame, (frame_features, key_index[:, 0]))
```

```python
import functools
import math

import jax
import jax.numpy as jnp
from jax import lax
from jax.experimental import pallas as pl
from jax.experimental.pallas import tpu as pltpu
from jax.sharding import PartitionSpec as P

MESH = pl.DeviceIdType.MESH
BF = jnp.bfloat16
F32 = jnp.float32

NF = 4
R = 4
X = 128
C = 128
H = NF * R
D = X + 16
E = X + 32
MSG = R * X + 128


def dot(a, b):
    return jnp.dot(a, b, preferred_element_type=F32)


def dot_t(a, b):
    return lax.dot_general(a, b, (((1,), (1,)), ((), ())), preferred_element_type=F32)


def kernel(
    ntm,
    ncol,
    kidx,
    feat,
    keys,
    mw,
    jw,
    dw,
    fw,
    out,
    F,
    KK,
    FE,
    ES_K,
    ES_F,
    EK,
    EF,
    SB,
    RB,
    PM,
    FQ,
    KR,
    CB,
    WB,
    J3,
    W1,
    H3,
    W2,
    HB,
    OS,
    RO,
    loc_sem,
    w_sem,
    ksend,
    krecv,
    esend,
    erecv,
    fsend,
    frecv,
    msend,
    mrecv,
    osend,
    orecv,
):
    tm = lax.axis_index("tm")
    row = lax.axis_index("row")
    col = lax.axis_index("col")
    nrow = NF
    tm_next = lax.rem(tm + 1, ntm)
    tm_prev = lax.rem(tm + ntm - 1, ntm)
    has_left = col > 0
    has_right = col < ncol - 1

    own_key = pltpu.make_async_copy(keys.at[0], KK.at[1], loc_sem.at[0])
    own_key.start()
    edge_l = pltpu.make_async_copy(feat.at[:, :, pl.ds(0, 16), :], FE.at[0], loc_sem.at[1])
    edge_l.start()
    edge_r = pltpu.make_async_copy(feat.at[:, :, pl.ds(X - 16, 16), :], FE.at[1], loc_sem.at[2])
    edge_r.start()
    own_feat = pltpu.make_async_copy(feat.at[row], F.at[row], loc_sem.at[3])
    own_feat.start()
    weights = []
    for i in range(3):
        for o in range(2):
            weights.append(
                pltpu.make_async_copy(jw.at[i], W1.at[i + o, :, pl.ds(128 * o, 128)], w_sem.at[0, i, o])
            )
            weights.append(
                pltpu.make_async_copy(dw.at[i], W2.at[i + o, :, pl.ds(128 * o, 128)], w_sem.at[1, i, o])
            )
    for w in weights:
        w.start()

    bar = pltpu.get_barrier_semaphore()

    def greet(t, r, c):
        pl.semaphore_signal(bar, inc=1, device_id=(t, r, c), device_id_type=MESH)

    for o in range(1, nrow):
        greet(tm, lax.rem(row + o, nrow), col)
    greet(tm_prev, row, col)

    @pl.when(has_left)
    def _():
        greet(tm, row, col - 1)
        greet(tm_prev, row, col - 1)

    @pl.when(has_right)
    def _():
        greet(tm, row, col + 1)
        greet(tm_prev, row, col + 1)

    pl.semaphore_wait(bar, nrow + 2 * has_left.astype(jnp.int32) + 2 * has_right.astype(jnp.int32))

    def remote(src, dst, s, r, dev):
        return pltpu.make_async_remote_copy(
            src_ref=src, dst_ref=dst, send_sem=s, recv_sem=r, device_id=dev, device_id_type=MESH
        )

    key_copy = remote(keys.at[0], KK.at[0], ksend, krecv, (tm_next, row, col))
    key_copy.start()
    feat_copies = []
    for o in (2, 1, 3):
        there = lax.rem(row + o, nrow)
        cp = remote(feat.at[there], F.at[row], fsend.at[o - 1], frecv.at[o - 1], (tm, there, col))
        cp.start()
        feat_copies.append(cp)

    own_key.wait()
    edge_l.wait()
    edge_r.wait()
    for side in range(2):
        kv = KK[1, :, X - 16 :, :] if side else KK[1, :, :16, :]
        kv = kv.astype(F32)[:, 8 * side : 8 * side + 8, :]
        ES_K[side] = kv.reshape(R * 8, C).astype(BF)
        for f in range(NF):
            fv = FE[side, f].astype(F32)[:, 8 * side : 8 * side + 8, :]
            ES_F[side, f] = fv.reshape(R * 8, C).astype(BF)

    def edge_copies(side):
        other = 1 - side
        c = col + 2 * side - 1
        return [
            remote(ES_K.at[side], EK.at[0, other], esend.at[side, 0], erecv.at[other, 0], (tm_next, row, c)),
            remote(ES_K.at[side], EK.at[1, other], esend.at[side, 1], erecv.at[other, 1], (tm, row, c)),
            remote(ES_F.at[side], EF.at[other], esend.at[side, 2], erecv.at[other, 2], (tm, row, c)),
        ]

    def edge_waits(side):
        c = col + 2 * side - 1
        return [
            remote(ES_K.at[side], EK.at[0, side], esend.at[side, 0], erecv.at[side, 0], (tm_next, row, c)),
            remote(ES_K.at[side], EK.at[1, side], esend.at[side, 1], erecv.at[side, 1], (tm, row, c)),
            remote(ES_F.at[side], EF.at[side], esend.at[side, 2], erecv.at[side, 2], (tm, row, c)),
        ]

    for side, has in ((0, has_left), (1, has_right)):

        @pl.when(has)
        def _(side=side):
            for cp in edge_copies(side):
                cp.start()

    q = lax.broadcasted_iota(jnp.int32, (144, 81), 0)
    d = lax.broadcasted_iota(jnp.int32, (144, 81), 1)
    t = q & 15
    pick = (d == 9 * (q >> 4) + 15 - t) & (t >= 7)
    WB[...] = jnp.zeros_like(WB)
    WB[176:320, :] = dot(pick.astype(F32).astype(BF), mw[...]).astype(BF)

    e = lax.broadcasted_iota(jnp.int32, (E, 192), 0)
    s = lax.broadcasted_iota(jnp.int32, (E, 192), 1)
    for yy in range(R):
        in_row = ((s >> 3) & 3) == yy
        x = jnp.where(s < X, s, jnp.where(s < X + 32, (s & 7) - 8, (s & 7) + X))
        keep = (x == 139 - e) & ((s < X) | in_row)
        PM[yy] = keep.astype(F32).astype(BF)

    zero = jnp.zeros((768, 128), BF)
    W1[0, :, 128:256] = zero
    W1[3, :, 0:128] = zero
    W2[0, :, 128:256] = zero[:384]
    W2[3, :, 0:128] = zero[:384]
    for i in (0, H + 1):
        J3[i] = jnp.zeros((D, 768), BF)
        HB[i] = jnp.zeros((X, 384), BF)
    for i in (0, 1, H + 2, H + 3):
        H3[i] = jnp.zeros((D, 384), BF)

    dd = lax.broadcasted_iota(jnp.int32, (D, C), 0)
    inside = (has_left | (dd >= 8)) & (has_right | (dd < X + 8))

    krecv_wait = remote(keys.at[0], KK.at[0], ksend, krecv, (tm_next, row, col))
    krecv_wait.wait()
    for side, has in ((0, has_left), (1, has_right)):

        @pl.when(has)
        def _(side=side):
            for cp in edge_waits(side):
                cp.wait_recv()

    def fill(dst, frame):
        slot = jnp.where(kidx[frame, 0] == tm, 1, 0)
        for yy in range(R):
            dst[X * yy : X * yy + X, :] = KK[slot, yy]
        for side in range(2):
            dst[R * X + 32 * side : R * X + 32 * side + 32, :] = EK[slot, side]
            dst[R * X + 64 + 32 * side : R * X + 96 + 32 * side, :] = EF[side, frame]

    msg_copies = []
    for o in (2, 1, 3):
        there = lax.rem(row + o, nrow)
        fill(SB.at[o - 1], there)
        cp = remote(SB.at[o - 1], RB.at[row], msend.at[o - 1], mrecv.at[o - 1], (tm, there, col))
        cp.start()
        msg_copies.append(cp)
    fill(RB.at[row], row)

    own_feat.wait()
    for cp in feat_copies:
        cp.wait_recv()
    for w in weights:
        w.wait()
    for cp in msg_copies:
        cp.wait_recv()

    hrow = lax.broadcasted_iota(jnp.int32, (64, C), 0)
    border = jnp.where(hrow < 32, has_left.astype(jnp.int32), has_right.astype(jnp.int32)) == 1

    def arrange(rs, carry):
        kh = jnp.where(border, RB[rs, R * X : R * X + 64, :].astype(F32), 0.0).astype(BF)
        fh = jnp.where(border, RB[rs, R * X + 64 : R * X + 128, :].astype(F32), 0.0)
        for yy in range(R):
            y = R * rs + yy
            src = jnp.concatenate([RB[rs, X * yy : X * yy + X, :], kh], axis=0)
            KR[y] = dot(PM[yy], src)
            fr = jnp.concatenate(
                [fh[8 * yy : 8 * yy + 8], F[rs, yy].astype(F32), fh[32 + 8 * yy : 40 + 8 * yy]], axis=0
            )
            FQ[y] = fr
            for j in range(3):
                sh = fr if j == 1 else pltpu.roll(fr, (1 - j) % D, 0)
                J3[y + 1, :, 256 * j + 128 : 256 * j + 256] = sh.astype(BF)
        return carry

    lax.fori_loop(0, NF, arrange, 0)

    scale = 1.0 / math.sqrt(C)

    def correlate(p, carry):
        parts = []
        for h in range(2):
            d0 = pl.multiple_of(16 * p + 8 * h, 8)
            e0 = pl.multiple_of(136 - 16 * p - 8 * h, 8)
            qs = FQ[:, pl.ds(d0, 8), :].reshape(H * 8, C).astype(BF)
            ks = KR[:, pl.ds(e0, 16), :].reshape(H * 16, C).astype(BF)
            sc = dot_t(qs, ks).reshape(H, 8, 256) * scale
            lo = pltpu.roll(sc[:, :, :128], 0, 2, stride=1, stride_axis=1)
            hi = pltpu.roll(sc[:, :, 128:], 0, 2, stride=1, stride_axis=1)
            parts.append(jnp.concatenate([lo, hi], axis=2))
        c0 = pl.multiple_of(16 * p, 16)
        CB[:, pl.ds(c0, 16), :] = jnp.concatenate(parts, axis=1).astype(BF)
        return carry

    lax.fori_loop(0, D // 16, correlate, 0)

    def motion(y, carry):
        w0 = pl.multiple_of(16 * (15 - y), 16)
        m = dot(CB[y], WB[pl.ds(w0, 256), :])
        m = jnp.where(inside, jnp.maximum(m, 0.0), 0.0)
        for j in range(3):
            sh = m if j == 1 else pltpu.roll(m, (1 - j) % D, 0)
            J3[y + 1, :, 256 * j : 256 * j + 128] = sh.astype(BF)
        return carry

    lax.fori_loop(0, H, motion, 0)

    def joint(p, carry):
        lhs = jnp.concatenate([J3[2 * p + t] for t in range(4)], axis=1)
        h = dot(lhs, W1[...].reshape(4 * 768, 256))
        for o in range(2):
            ho = jnp.where(inside, jnp.maximum(h[:, 128 * o : 128 * o + 128], 0.0), 0.0)
            for j in range(3):
                sh = ho if j == 1 else pltpu.roll(ho, (2 - 2 * j) % D, 0)
                H3[2 * p + o + 2, :, 128 * j : 128 * j + 128] = sh.astype(BF)
        return carry

    lax.fori_loop(0, H // 2, joint, 0)

    def dilated(p, carry):
        y0 = 4 * (p // 2) + lax.rem(p, 2)
        lhs = jnp.concatenate([H3[y0 + 2 * t] for t in range(4)], axis=1)
        h = dot(lhs, W2[...].reshape(4 * 384, 256))
        for o in range(2):
            ho = jnp.where(inside, jnp.maximum(h[:, 128 * o : 128 * o + 128], 0.0), 0.0)
            for j in range(3):
                sh = pltpu.roll(ho, (-7 - j) % D, 0)[:X]
                HB[y0 + 2 * o + 1, :, 128 * j : 128 * j + 128] = sh.astype(BF)
        return carry

    lax.fori_loop(0, H // 2, dilated, 0)

    def head(rr, carry):
        for yy in range(R):
            y = R * rr + yy
            rhs = jnp.concatenate([HB[y + i] for i in range(3)], axis=1)
            res = dot_t(fw[...], rhs)
            OS[rr, :, yy : yy + 1, :] = res.reshape(2, 1, X)
        return carry

    lax.fori_loop(0, NF, head, 0)

    out_copies = []
    for o in range(1, nrow):
        there = lax.rem(row + o, nrow)
        cp = remote(OS.at[there], RO.at[row], osend.at[o - 1], orecv.at[o - 1], (tm, there, col))
        cp.start()
        out_copies.append(cp)
    RO[row] = OS[row]
    for cp in out_copies:
        cp.wait_recv()
    out[...] = RO[...]

    for cp in feat_copies + msg_copies + out_copies:
        cp.wait_send()
    for side, has in ((0, has_left), (1, has_right)):

        @pl.when(has)
        def _(side=side):
            for cp in edge_copies(side):
                cp.wait_send()


def solution(mesh):
    ntm, ncol = mesh.shape["tm"], mesh.shape["col"]

    def step(feat, keys, kidx, mw, jw, dw, fw):
        anyspec = pl.BlockSpec(memory_space=pltpu.HBM)
        vspec = pl.BlockSpec(memory_space=pltpu.VMEM)
        dma = pltpu.SemaphoreType.DMA
        return pl.pallas_call(
            functools.partial(kernel, ntm, ncol),
            out_shape=jax.ShapeDtypeStruct((NF, 2, R, X), F32),
            in_specs=[
                pl.BlockSpec(memory_space=pltpu.SMEM),
                anyspec,
                anyspec,
                vspec,
                anyspec,
                anyspec,
                vspec,
            ],
            out_specs=vspec,
            scratch_shapes=[
                pltpu.VMEM((NF, R, X, C), BF),
                pltpu.VMEM((2, R, X, C), BF),
                pltpu.VMEM((2, NF, R, 16, C), BF),
                pltpu.VMEM((2, R * 8, C), BF),
                pltpu.VMEM((2, NF, R * 8, C), BF),
                pltpu.VMEM((2, 2, R * 8, C), BF),
                pltpu.VMEM((2, NF, R * 8, C), BF),
                pltpu.VMEM((3, MSG, C), BF),
                pltpu.VMEM((NF, MSG, C), BF),
                pltpu.VMEM((R, E, 192), BF),
                pltpu.VMEM((H, D, C), F32),
                pltpu.VMEM((H, E, C), F32),
                pltpu.VMEM((H, D, 256), BF),
                pltpu.VMEM((31 * 16, C), BF),
                pltpu.VMEM((H + 2, D, 768), BF),
                pltpu.VMEM((4, 768, 256), BF),
                pltpu.VMEM((H + 4, D, 384), BF),
                pltpu.VMEM((4, 384, 256), BF),
                pltpu.VMEM((H + 2, X, 384), BF),
                pltpu.VMEM((NF, 2, R, X), F32),
                pltpu.VMEM((NF, 2, R, X), F32),
                dma((4,)),
                dma((2, 3, 2)),
                dma,
                dma,
                dma((2, 3)),
                dma((2, 3)),
                dma((3,)),
                dma((3,)),
                dma((3,)),
                dma((3,)),
                dma((3,)),
                dma((3,)),
            ],
            compiler_params=pltpu.CompilerParams(
                collective_id=0, has_side_effects=True, vmem_limit_bytes=48 * 1024 * 1024
            ),
        )(
            kidx,
            feat,
            keys,
            mw,
            jw.reshape(3, 768, 128),
            dw.reshape(3, 384, 128),
            fw.reshape(2, 1152),
        )

    in_specs = (
        P("tm", "row", "col", None),
        P("tm", "row", "col", None),
        P("tm", None),
        P(),
        P(),
        P(),
        P(),
    )
    return jax.shard_map(
        step, mesh=mesh, in_specs=in_specs, out_specs=P("tm", None, "row", "col"), check_vma=False
    )
```

```python
import functools
import math

import jax
import jax.numpy as jnp
from jax import lax
from jax.experimental import pallas as pl
from jax.experimental.pallas import tpu as pltpu
from jax.sharding import PartitionSpec as P

MESH = pl.DeviceIdType.MESH
BF = jnp.bfloat16
F32 = jnp.float32

NF = 4
R = 4
X = 128
C = 128
H = NF * R
D = X + 16
E = X + 32
MSG = R * X


def dot(a, b):
    return jnp.dot(a, b, preferred_element_type=F32)


def dot_t(a, b):
    return lax.dot_general(a, b, (((1,), (1,)), ((), ())), preferred_element_type=F32)


def kernel(
    ntm,
    ncol,
    kidx,
    feat,
    keys,
    mw,
    jw,
    dw,
    fw,
    out,
    F,
    KK,
    FE,
    ES_K,
    ES_F,
    EK,
    EF,
    SB,
    RB,
    SH,
    RH,
    MW,
    FW,
    PM,
    FQ,
    KR,
    CB,
    WB,
    J3,
    W1,
    H3,
    W2,
    HB,
    OS,
    RO,
    loc_sem,
    w_sem,
    ksend,
    krecv,
    esend,
    erecv,
    fsend,
    frecv,
    msend,
    mrecv,
    hsend,
    hrecv,
    ready,
    osend,
    orecv,
):
    tm = lax.axis_index("tm")
    row = lax.axis_index("row")
    col = lax.axis_index("col")
    nrow = NF
    tm_next = lax.rem(tm + 1, ntm)
    tm_prev = lax.rem(tm + ntm - 1, ntm)
    has_left = col > 0
    has_right = col < ncol - 1

    def local(src, dst, sem):
        cp = pltpu.make_async_copy(src, dst, sem)
        cp.start()
        return cp

    cross_left = has_left & (lax.rem(col, 2) == 0)
    cross_right = has_right & (lax.rem(col, 2) == 1)
    near_left = has_left & (lax.rem(col, 2) == 1)
    near_right = has_right & (lax.rem(col, 2) == 0)

    bar = pltpu.get_barrier_semaphore()

    def greet(t, r, c):
        pl.semaphore_signal(bar, inc=1, device_id=(t, r, c), device_id_type=MESH)

    for o in range(1, nrow):
        greet(tm, lax.rem(row + o, nrow), col)
    greet(tm_prev, row, col)

    @pl.when(cross_right)
    def _():
        greet(tm, row, col + 1)
        greet(tm_prev, row, col + 1)
        greet(tm_next, row, col + 1)

    @pl.when(near_left)
    def _():
        greet(tm, row, col - 1)
        greet(tm_prev, row, col - 1)

    @pl.when(near_right)
    def _():
        greet(tm, row, col + 1)
        greet(tm_prev, row, col + 1)

    own_key = local(keys.at[0], KK.at[1], loc_sem.at[0])
    edge_l = local(feat.at[:, :, pl.ds(0, 16), :], FE.at[0], loc_sem.at[1])
    edge_r = local(feat.at[:, :, pl.ds(X - 16, 16), :], FE.at[1], loc_sem.at[2])
    own_feat = local(feat.at[row], F.at[row], loc_sem.at[3])
    weights = [local(mw, MW, loc_sem.at[4]), local(fw, FW, loc_sem.at[5])]
    for i in range(3):
        for o in range(2):
            weights.append(local(jw.at[i], W1.at[i + o, :, pl.ds(128 * o, 128)], w_sem.at[0, i, o]))
            weights.append(local(dw.at[i], W2.at[i + o, :, pl.ds(128 * o, 128)], w_sem.at[1, i, o]))

    own_key.wait()
    edge_l.wait()
    edge_r.wait()
    for side in range(2):
        kv = KK[1, :, X - 16 :, :] if side else KK[1, :, :16, :]
        kv = kv.astype(F32)[:, 8 * side : 8 * side + 8, :]
        ES_K[side] = kv.reshape(R * 8, C).astype(BF)
        for f in range(NF):
            fv = FE[side, f].astype(F32)[:, 8 * side : 8 * side + 8, :]
            ES_F[side, f] = fv.reshape(R * 8, C).astype(BF)

    one = lambda flag, n: n * flag.astype(jnp.int32)
    pl.semaphore_wait(bar, nrow + one(near_left, 2) + one(near_right, 2) + one(cross_left, 3))

    @pl.when(cross_left)
    def _():
        for t in (tm, tm_prev):
            pl.semaphore_signal(ready, inc=1, device_id=(t, row, col - 1), device_id_type=MESH)

    def remote(src, dst, s, r, dev):
        return pltpu.make_async_remote_copy(
            src_ref=src, dst_ref=dst, send_sem=s, recv_sem=r, device_id=dev, device_id_type=MESH
        )

    def edge_copies(side):
        other = 1 - side
        c = col + 2 * side - 1
        return [
            remote(ES_K.at[side], EK.at[0, other], esend.at[side, 0], erecv.at[other, 0], (tm_next, row, c)),
            remote(ES_K.at[side], EK.at[1, other], esend.at[side, 1], erecv.at[other, 1], (tm, row, c)),
            remote(ES_F.at[side], EF.at[other], esend.at[side, 2], erecv.at[other, 2], (tm, row, c)),
        ]

    def edge_waits(side):
        c = col + 2 * side - 1
        return [
            remote(ES_K.at[side], EK.at[0, side], esend.at[side, 0], erecv.at[side, 0], (tm_next, row, c)),
            remote(ES_K.at[side], EK.at[1, side], esend.at[side, 1], erecv.at[side, 1], (tm, row, c)),
            remote(ES_F.at[side], EF.at[side], esend.at[side, 2], erecv.at[side, 2], (tm, row, c)),
        ]

    for side, go in ((0, has_left), (1, near_right)):

        @pl.when(go)
        def _(side=side):
            for cp in edge_copies(side):
                cp.start()

    key_copy = remote(keys.at[0], KK.at[0], ksend, krecv, (tm_next, row, col))
    key_copy.start()
    feat_copies = []
    for o in (2, 1, 3):
        there = lax.rem(row + o, nrow)
        cp = remote(feat.at[there], F.at[row], fsend.at[o - 1], frecv.at[o - 1], (tm, there, col))
        cp.start()
        feat_copies.append(cp)

    for w in weights:
        w.wait()
    q = lax.broadcasted_iota(jnp.int32, (144, 81), 0)
    d = lax.broadcasted_iota(jnp.int32, (144, 81), 1)
    t = q & 15
    pick = (d == 9 * (q >> 4) + 15 - t) & (t >= 7)
    WB[...] = jnp.zeros_like(WB)
    WB[176:320, :] = dot(pick.astype(F32).astype(BF), MW[...]).astype(BF)

    e = lax.broadcasted_iota(jnp.int32, (E, 192), 0)
    s = lax.broadcasted_iota(jnp.int32, (E, 192), 1)
    for yy in range(R):
        in_row = ((s >> 3) & 3) == yy
        x = jnp.where(s < X, s, jnp.where(s < X + 32, (s & 7) - 8, (s & 7) + X))
        keep = (x == 139 - e) & ((s < X) | in_row)
        PM[yy] = keep.astype(F32).astype(BF)

    zero = jnp.zeros((768, 128), BF)
    W1[0, :, 128:256] = zero
    W1[3, :, 0:128] = zero
    W2[0, :, 128:256] = zero[:384]
    W2[3, :, 0:128] = zero[:384]
    for i in (0, H + 1):
        J3[i] = jnp.zeros((D, 768), BF)
        HB[i] = jnp.zeros((X, 384), BF)
    for i in (0, 1, H + 2, H + 3):
        H3[i] = jnp.zeros((D, 384), BF)

    dd = lax.broadcasted_iota(jnp.int32, (D, C), 0)
    inside = (has_left | (dd >= 8)) & (has_right | (dd < X + 8))

    key_copy.wait()

    def slot_of(frame):
        return jnp.where(kidx[frame] == tm, 1, 0)

    def fill(dst, frame):
        slot = slot_of(frame)
        for yy in range(R):
            dst[X * yy : X * yy + X, :] = KK[slot, yy]

    def fill_border(dst, frame):
        slot = slot_of(frame)
        for side in range(2):
            dst[32 * side : 32 * side + 32, :] = EK[slot, side]
            dst[64 + 32 * side : 96 + 32 * side, :] = EF[side, frame]

    msg_copies = []
    for o in (2, 1, 3):
        there = lax.rem(row + o, nrow)
        fill(SB.at[o - 1], there)
        cp = remote(SB.at[o - 1], RB.at[row], msend.at[o - 1], mrecv.at[o - 1], (tm, there, col))
        cp.start()
        msg_copies.append(cp)
    fill(RB.at[row], row)

    @pl.when(cross_right)
    def _():
        pl.semaphore_wait(ready, 2)
        for cp in edge_copies(1):
            cp.start()

    for side, has in ((0, has_left), (1, has_right)):

        @pl.when(has)
        def _(side=side):
            for cp in edge_waits(side):
                cp.wait_recv()

    border_copies = []
    for o in (2, 1, 3):
        there = lax.rem(row + o, nrow)
        fill_border(SH.at[o - 1], there)
        cp = remote(SH.at[o - 1], RH.at[row], hsend.at[o - 1], hrecv.at[o - 1], (tm, there, col))
        cp.start()
        border_copies.append(cp)
    fill_border(RH.at[row], row)

    own_feat.wait()
    for cp in feat_copies + msg_copies + border_copies:
        cp.wait_recv()

    hrow = lax.broadcasted_iota(jnp.int32, (64, C), 0)
    border = jnp.where(hrow < 32, has_left.astype(jnp.int32), has_right.astype(jnp.int32)) == 1

    def arrange(rs, carry):
        kh = jnp.where(border, RH[rs, :64, :].astype(F32), 0.0).astype(BF)
        fh = jnp.where(border, RH[rs, 64:, :].astype(F32), 0.0)
        for yy in range(R):
            y = R * rs + yy
            src = jnp.concatenate([RB[rs, X * yy : X * yy + X, :], kh], axis=0)
            KR[y] = dot(PM[yy], src)
            fr = jnp.concatenate(
                [fh[8 * yy : 8 * yy + 8], F[rs, yy].astype(F32), fh[32 + 8 * yy : 40 + 8 * yy]], axis=0
            )
            FQ[y] = fr
            for j in range(3):
                sh = fr if j == 1 else pltpu.roll(fr, (1 - j) % D, 0)
                J3[y + 1, :, 256 * j + 128 : 256 * j + 256] = sh.astype(BF)
        return carry

    lax.fori_loop(0, NF, arrange, 0)

    scale = 1.0 / math.sqrt(C)

    def correlate(p, carry):
        parts = []
        for h in range(2):
            d0 = pl.multiple_of(16 * p + 8 * h, 8)
            e0 = pl.multiple_of(136 - 16 * p - 8 * h, 8)
            qs = FQ[:, pl.ds(d0, 8), :].reshape(H * 8, C).astype(BF)
            ks = KR[:, pl.ds(e0, 16), :].reshape(H * 16, C).astype(BF)
            sc = dot_t(qs, ks).reshape(H, 8, 256) * scale
            lo = pltpu.roll(sc[:, :, :128], 0, 2, stride=1, stride_axis=1)
            hi = pltpu.roll(sc[:, :, 128:], 0, 2, stride=1, stride_axis=1)
            parts.append(jnp.concatenate([lo, hi], axis=2))
        c0 = pl.multiple_of(16 * p, 16)
        CB[:, pl.ds(c0, 16), :] = jnp.concatenate(parts, axis=1).astype(BF)
        return carry

    lax.fori_loop(0, D // 16, correlate, 0)

    def motion(y, carry):
        w0 = pl.multiple_of(16 * (15 - y), 16)
        m = dot(CB[y], WB[pl.ds(w0, 256), :])
        m = jnp.where(inside, jnp.maximum(m, 0.0), 0.0)
        for j in range(3):
            sh = m if j == 1 else pltpu.roll(m, (1 - j) % D, 0)
            J3[y + 1, :, 256 * j : 256 * j + 128] = sh.astype(BF)
        return carry

    lax.fori_loop(0, H, motion, 0)

    def joint(p, carry):
        lhs = jnp.concatenate([J3[2 * p + t] for t in range(4)], axis=1)
        h = dot(lhs, W1[...].reshape(4 * 768, 256))
        for o in range(2):
            ho = jnp.where(inside, jnp.maximum(h[:, 128 * o : 128 * o + 128], 0.0), 0.0)
            for j in range(3):
                sh = ho if j == 1 else pltpu.roll(ho, (2 - 2 * j) % D, 0)
                H3[2 * p + o + 2, :, 128 * j : 128 * j + 128] = sh.astype(BF)
        return carry

    lax.fori_loop(0, H // 2, joint, 0)

    def dilated(p, carry):
        y0 = 4 * (p // 2) + lax.rem(p, 2)
        lhs = jnp.concatenate([H3[y0 + 2 * t] for t in range(4)], axis=1)
        h = dot(lhs, W2[...].reshape(4 * 384, 256))
        for o in range(2):
            ho = jnp.where(inside, jnp.maximum(h[:, 128 * o : 128 * o + 128], 0.0), 0.0)
            for j in range(3):
                sh = pltpu.roll(ho, (-7 - j) % D, 0)[:X]
                HB[y0 + 2 * o + 1, :, 128 * j : 128 * j + 128] = sh.astype(BF)
        return carry

    lax.fori_loop(0, H // 2, dilated, 0)

    def head(rr, carry):
        for yy in range(R):
            y = R * rr + yy
            rhs = jnp.concatenate([HB[y + i] for i in range(3)], axis=1)
            res = dot_t(FW[...], rhs)
            OS[rr, :, yy : yy + 1, :] = res.reshape(2, 1, X)
        return carry

    lax.fori_loop(0, NF, head, 0)

    out_copies = []
    for o in range(1, nrow):
        there = lax.rem(row + o, nrow)
        cp = remote(OS.at[there], RO.at[row], osend.at[o - 1], orecv.at[o - 1], (tm, there, col))
        cp.start()
        out_copies.append(cp)
    RO[row] = OS[row]
    for cp in out_copies:
        cp.wait_recv()
    out[...] = RO[...]

    for cp in feat_copies + msg_copies + border_copies + out_copies:
        cp.wait_send()
    for side, has in ((0, has_left), (1, has_right)):

        @pl.when(has)
        def _(side=side):
            for cp in edge_copies(side):
                cp.wait_send()


def solution(mesh):
    ntm, ncol = mesh.shape["tm"], mesh.shape["col"]

    def step(feat, keys, kidx, mw, jw, dw, fw):
        anyspec = pl.BlockSpec(memory_space=pltpu.HBM)
        vspec = pl.BlockSpec(memory_space=pltpu.VMEM)
        dma = pltpu.SemaphoreType.DMA
        return pl.pallas_call(
            functools.partial(kernel, ntm, ncol),
            out_shape=jax.ShapeDtypeStruct((NF, 2, R, X), F32),
            in_specs=[
                pl.BlockSpec(memory_space=pltpu.SMEM),
                anyspec,
                anyspec,
                anyspec,
                anyspec,
                anyspec,
                anyspec,
            ],
            out_specs=vspec,
            scratch_shapes=[
                pltpu.VMEM((NF, R, X, C), BF),
                pltpu.VMEM((2, R, X, C), BF),
                pltpu.VMEM((2, NF, R, 16, C), BF),
                pltpu.VMEM((2, R * 8, C), BF),
                pltpu.VMEM((2, NF, R * 8, C), BF),
                pltpu.VMEM((2, 2, R * 8, C), BF),
                pltpu.VMEM((2, NF, R * 8, C), BF),
                pltpu.VMEM((3, MSG, C), BF),
                pltpu.VMEM((NF, MSG, C), BF),
                pltpu.VMEM((3, 128, C), BF),
                pltpu.VMEM((NF, 128, C), BF),
                pltpu.VMEM((81, C), BF),
                pltpu.VMEM((2, 9 * C), BF),
                pltpu.VMEM((R, E, 192), BF),
                pltpu.VMEM((H, D, C), F32),
                pltpu.VMEM((H, E, C), F32),
                pltpu.VMEM((H, D, 256), BF),
                pltpu.VMEM((31 * 16, C), BF),
                pltpu.VMEM((H + 2, D, 768), BF),
                pltpu.VMEM((4, 768, 256), BF),
                pltpu.VMEM((H + 4, D, 384), BF),
                pltpu.VMEM((4, 384, 256), BF),
                pltpu.VMEM((H + 2, X, 384), BF),
                pltpu.VMEM((NF, 2, R, X), F32),
                pltpu.VMEM((NF, 2, R, X), F32),
                dma((6,)),
                dma((2, 3, 2)),
                dma,
                dma,
                dma((2, 3)),
                dma((2, 3)),
                dma((3,)),
                dma((3,)),
                dma((3,)),
                dma((3,)),
                dma((3,)),
                dma((3,)),
                pltpu.SemaphoreType.REGULAR,
                dma((3,)),
                dma((3,)),
            ],
            compiler_params=pltpu.CompilerParams(
                collective_id=0, has_side_effects=True, vmem_limit_bytes=60 * 1024 * 1024
            ),
        )(
            kidx.reshape(NF),
            feat,
            keys,
            mw,
            jw.reshape(3, 768, 128),
            dw.reshape(3, 384, 128),
            fw.reshape(2, 1152),
        )

    in_specs = (
        P("tm", "row", "col", None),
        P("tm", "row", "col", None),
        P("tm", None),
        P(),
        P(),
        P(),
        P(),
    )
    return jax.shard_map(
        step, mesh=mesh, in_specs=in_specs, out_specs=P("tm", None, "row", "col"), check_vma=False
    )
```

```python
import functools
import math

import jax
import jax.numpy as jnp
from jax import lax
from jax.experimental import pallas as pl
from jax.experimental.pallas import tpu as pltpu
from jax.sharding import PartitionSpec as P

MESH = pl.DeviceIdType.MESH
BF = jnp.bfloat16
F32 = jnp.float32

NF = 4
R = 4
X = 128
C = 128
H = NF * R
D = X + 16
E = X + 32
NCH = 4
CH = X // NCH


def dot(a, b):
    return jnp.dot(a, b, preferred_element_type=F32)


def dot_t(a, b):
    return lax.dot_general(a, b, (((1,), (1,)), ((), ())), preferred_element_type=F32)


def kernel(
    ntm,
    ncol,
    kidx,
    feat,
    keys,
    mw,
    jw,
    dw,
    fw,
    out,
    F,
    KK,
    KV,
    FE,
    ES_K,
    ES_F,
    EK,
    EF,
    SB,
    RB,
    SH,
    RH,
    MW,
    FW,
    FQ,
    KR,
    CB,
    WR,
    MF,
    JF,
    JM,
    WF,
    WM,
    HF,
    H3,
    W2,
    W4,
    RS,
    OS,
    RO,
    loc_sem,
    w_sem,
    ksend,
    krecv,
    esend,
    erecv,
    fsend,
    frecv,
    msend,
    mrecv,
    osend,
    orecv,
    ready,
    hsend,
    hrecv,
):
    tm = lax.axis_index("tm")
    row = lax.axis_index("row")
    col = lax.axis_index("col")
    nrow = NF
    tm_next = lax.rem(tm + 1, ntm)
    tm_prev = lax.rem(tm + ntm - 1, ntm)
    has_left = col > 0
    has_right = col < ncol - 1

    def local(src, dst, sem):
        cp = pltpu.make_async_copy(src, dst, sem)
        cp.start()
        return cp

    cross_left = has_left & (lax.rem(col, 2) == 0)
    cross_right = has_right & (lax.rem(col, 2) == 1)
    near_left = has_left & (lax.rem(col, 2) == 1)
    near_right = has_right & (lax.rem(col, 2) == 0)

    bar = pltpu.get_barrier_semaphore()

    def greet(t, r, c):
        pl.semaphore_signal(bar, inc=1, device_id=(t, r, c), device_id_type=MESH)

    for o in range(1, nrow):
        greet(tm, lax.rem(row + o, nrow), col)
    greet(tm_prev, row, col)

    @pl.when(cross_right)
    def _():
        greet(tm, row, col + 1)
        greet(tm_prev, row, col + 1)
        greet(tm_next, row, col + 1)

    @pl.when(near_left)
    def _():
        greet(tm, row, col - 1)
        greet(tm_prev, row, col - 1)

    @pl.when(near_right)
    def _():
        greet(tm, row, col + 1)
        greet(tm_prev, row, col + 1)

    own_key = local(keys.at[0], KV, loc_sem.at[0])
    edge_l = local(feat.at[:, :, pl.ds(0, 16), :], FE.at[0], loc_sem.at[1])
    edge_r = local(feat.at[:, :, pl.ds(X - 16, 16), :], FE.at[1], loc_sem.at[2])
    own_feat = local(feat.at[row], F.at[row], loc_sem.at[3])
    weights = [local(mw, MW, loc_sem.at[4]), local(fw, FW, loc_sem.at[5])]
    for i in range(3):
        for o in range(2):
            half = pl.ds(128 * o, 128)
            weights.append(local(jw.at[i, :, pl.ds(0, C), :], WM.at[i + o, :, :, half], w_sem.at[0, i, o]))
            weights.append(local(jw.at[i, :, pl.ds(C, C), :], WF.at[i + o, :, :, half], w_sem.at[1, i, o]))
            weights.append(local(dw.at[i], W2.at[i + o, :, half], w_sem.at[2, i, o]))

    own_key.wait()
    ri = lax.broadcasted_iota(jnp.int32, (X, X), 0)
    ci = lax.broadcasted_iota(jnp.int32, (X, X), 1)
    turn = (ri + ci == X - 1).astype(F32).astype(BF)
    for yy in range(R):
        KK[1, yy] = dot(turn, KV[yy]).astype(BF)

    edge_l.wait()
    edge_r.wait()
    for side in range(2):
        kv = KK[1, :, :16, :].astype(F32)[:, :8, :] if side else KK[1, :, X - 16 :, :].astype(F32)[:, 8:, :]
        ES_K[side] = kv.reshape(R * 8, C).astype(BF)
        for f in range(NF):
            fv = FE[side, f].astype(F32)[:, 8 * side : 8 * side + 8, :]
            ES_F[side, f] = fv.reshape(R * 8, C).astype(BF)

    one = lambda flag, n: n * flag.astype(jnp.int32)
    pl.semaphore_wait(bar, nrow + one(near_left, 2) + one(near_right, 2) + one(cross_left, 3))

    @pl.when(cross_left)
    def _():
        for t in (tm, tm_prev):
            pl.semaphore_signal(ready, inc=1, device_id=(t, row, col - 1), device_id_type=MESH)

    def remote(src, dst, s, r, dev):
        return pltpu.make_async_remote_copy(
            src_ref=src, dst_ref=dst, send_sem=s, recv_sem=r, device_id=dev, device_id_type=MESH
        )

    def edge_copies(side):
        other = 1 - side
        c = col + 2 * side - 1
        return [
            remote(ES_K.at[side], EK.at[0, other], esend.at[side, 0], erecv.at[other, 0], (tm_next, row, c)),
            remote(ES_K.at[side], EK.at[1, other], esend.at[side, 1], erecv.at[other, 1], (tm, row, c)),
            remote(ES_F.at[side], EF.at[other], esend.at[side, 2], erecv.at[other, 2], (tm, row, c)),
        ]

    def edge_waits(side):
        c = col + 2 * side - 1
        return [
            remote(ES_K.at[side], EK.at[0, side], esend.at[side, 0], erecv.at[side, 0], (tm_next, row, c)),
            remote(ES_K.at[side], EK.at[1, side], esend.at[side, 1], erecv.at[side, 1], (tm, row, c)),
            remote(ES_F.at[side], EF.at[side], esend.at[side, 2], erecv.at[side, 2], (tm, row, c)),
        ]

    for side, go in ((0, has_left), (1, near_right)):

        @pl.when(go)
        def _(side=side):
            for cp in edge_copies(side):
                cp.start()

    key_copy = remote(KK.at[1], KK.at[0], ksend, krecv, (tm_next, row, col))
    key_copy.start()
    feat_copies = []
    for o in (2, 1, 3):
        there = lax.rem(row + o, nrow)
        cp = remote(feat.at[there], F.at[row], fsend.at[o - 1], frecv.at[o - 1], (tm, there, col))
        cp.start()
        feat_copies.append(cp)

    for w in weights:
        w.wait()
    q = lax.broadcasted_iota(jnp.int32, (256, 81), 0)
    d = lax.broadcasted_iota(jnp.int32, (256, 81), 1)
    t = q & 15
    pick = (d == 9 * (q >> 4) + 15 - t) & (t >= 7) & (q < 144)
    WR[...] = dot(pick.astype(F32).astype(BF), MW[...]).astype(BF)

    zero = jnp.zeros((3, 128, 128), BF)
    for w in (WM, WF):
        w[0, :, :, 128:256] = zero
        w[3, :, :, 0:128] = zero
    W2[0, :, 128:256] = zero.reshape(384, 128)
    W2[3, :, 0:128] = zero.reshape(384, 128)
    for i in range(3):
        W4[2 * i : 2 * i + 2, :] = FW[:, 384 * i : 384 * i + 384].astype(F32)
    W4[6:8, :] = jnp.zeros((2, 384), F32)
    for i in (0, H + 1):
        JF[i] = jnp.zeros((D, 384), BF)
        JM[i] = jnp.zeros((D, 384), BF)
        RS[i] = jnp.zeros((8, X), F32)
    for i in (0, 1, H + 2, H + 3):
        H3[i] = jnp.zeros((D, 384), BF)
    KR[:, 0:8, :] = jnp.zeros((H, 8, C), F32)
    KR[:, E - 16 :, :] = jnp.zeros((H, 16, C), F32)
    MF[:, 0:8, :] = jnp.zeros((H, 8, C), F32)
    MF[:, D + 8 :, :] = jnp.zeros((H, 8, C), F32)

    dd = lax.broadcasted_iota(jnp.int32, (D, C), 0)
    inside = (has_left | (dd >= 8)) & (has_right | (dd < X + 8))

    key_copy.wait()

    def slot_of(frame):
        return jnp.where(kidx[frame] == tm, 1, 0)

    def fill_border(dst, frame):
        slot = slot_of(frame)
        for side in range(2):
            dst[32 * side : 32 * side + 32, :] = EK[slot, side]
            dst[64 + 32 * side : 96 + 32 * side, :] = EF[side, frame]

    slots = [slot_of(lax.rem(row + o, nrow)) for o in range(nrow)]
    msg_copies = []
    for k in range(NCH):
        part = slice(X - (k + 1) * CH, X - k * CH)
        ds = pl.ds(X - (k + 1) * CH, CH)
        copies = []
        for o in (2, 1, 3):
            there = lax.rem(row + o, nrow)
            SB[o - 1, :, part, :] = KK[slots[o], :, part, :]
            cp = remote(
                SB.at[o - 1, :, ds, :], RB.at[row, :, ds, :], msend.at[k, o - 1], mrecv.at[k, o - 1], (tm, there, col)
            )
            cp.start()
            copies.append(cp)
        msg_copies.append(copies)
    RB[row] = KK[slots[0]]

    @pl.when(cross_right)
    def _():
        pl.semaphore_wait(ready, 2)
        for cp in edge_copies(1):
            cp.start()

    for side, has in ((0, has_left), (1, has_right)):

        @pl.when(has)
        def _(side=side):
            for cp in edge_waits(side):
                cp.wait_recv()

    border_copies = []
    for o in (2, 1, 3):
        there = lax.rem(row + o, nrow)
        fill_border(SH.at[o - 1], there)
        cp = remote(SH.at[o - 1], RH.at[row], hsend.at[o - 1], hrecv.at[o - 1], (tm, there, col))
        cp.start()
        border_copies.append(cp)
    fill_border(RH.at[row], row)

    own_feat.wait()
    for cp in feat_copies + border_copies:
        cp.wait_recv()

    hrow = lax.broadcasted_iota(jnp.int32, (64, C), 0)
    border = jnp.where(hrow < 32, has_left.astype(jnp.int32), has_right.astype(jnp.int32)) == 1

    def arrange(rs, carry):
        kh = jnp.where(border, RH[rs, :64, :].astype(F32), 0.0)
        fh = jnp.where(border, RH[rs, 64:, :].astype(F32), 0.0)
        for yy in range(R):
            y = R * rs + yy
            KR[y, 140:148, :] = kh[8 * yy : 8 * yy + 8]
            KR[y, 4:12, :] = kh[32 + 8 * yy : 40 + 8 * yy]
            fr = jnp.concatenate(
                [fh[8 * yy : 8 * yy + 8], F[rs, yy].astype(F32), fh[32 + 8 * yy : 40 + 8 * yy]], axis=0
            )
            FQ[y] = fr
            for j in range(3):
                sh = fr if j == 1 else pltpu.roll(fr, (1 - j) % D, 0)
                JF[y + 1, :, 128 * j : 128 * j + 128] = sh.astype(BF)
        return carry

    lax.fori_loop(0, NF, arrange, 0)

    def pairs(src, first, gap):
        return jnp.concatenate(
            [
                jnp.concatenate([src[first + t * (3 - gap)] for t in range(4)], axis=1),
                jnp.concatenate([src[first + gap + t * (3 - gap)] for t in range(4)], axis=1),
            ],
            axis=0,
        )

    def joint_frames(p, carry):
        HF[p] = dot(pairs(JF, 4 * p, 2), WF[...].reshape(1536, 256))
        return carry

    lax.fori_loop(0, H // 4, joint_frames, 0)

    scale = 1.0 / math.sqrt(C)
    lane = lax.broadcasted_iota(jnp.int32, (8, 128), 1)

    def correlate(p, carry):
        parts = [[], []]
        for h in range(2):
            d0 = pl.multiple_of(16 * p + 8 * h, 8)
            e0 = pl.multiple_of(136 - 16 * p - 8 * h, 8)
            qs = FQ[:, pl.ds(d0, 8), :].reshape(H * 8, C).astype(BF)
            ks = KR[:, pl.ds(e0, 16), :].reshape(H * 16, C).astype(BF)
            sc = (dot_t(qs, ks) * scale).reshape(H, 8, 256)
            for y in range(H):
                turn = (64 - 16 * y) % 256
                by = turn % 128
                lo = pltpu.roll(sc[y, :, :128], by, 1, stride=1, stride_axis=0)
                hi = pltpu.roll(sc[y, :, 128:], by, 1, stride=1, stride_axis=0)
                if turn >= 128:
                    lo, hi = hi, lo
                low = jnp.where(lane < by, hi, lo) if by else lo
                high = jnp.where(lane < by, lo, hi) if by else hi
                if y < 4:
                    low = jnp.where(lane >= 16 * (4 - y), low, 0.0)
                if y > 11:
                    high = jnp.zeros_like(high)
                if y > 12:
                    low = jnp.where(lane < 16 * (20 - y), low, 0.0)
                parts[h].append(jnp.concatenate([low, high], axis=1))
        c0 = pl.multiple_of(16 * p, 16)
        for y in range(H):
            CB[y, pl.ds(c0, 16), :] = jnp.concatenate([parts[0][y], parts[1][y]], axis=0).astype(BF)
        return carry

    done = 0
    for k in range(NCH):
        for cp in msg_copies[k]:
            cp.wait_recv()
        s0 = X - (k + 1) * CH

        def place(rs, carry, s0=s0):
            y0 = R * rs
            for yy in range(R):
                KR[y0 + yy, 12 + s0 : 12 + s0 + CH, :] = RB[rs, yy, s0 : s0 + CH, :].astype(F32)
            return carry

        lax.fori_loop(0, NF, place, 0)
        upto = D // 16 if k == NCH - 1 else ((k + 1) * CH - 12) // 16 + 1
        lax.fori_loop(done, upto, correlate, 0)
        n = 16 * (upto - done)
        d0 = 16 * done
        m = dot(CB[:, d0 : d0 + n, :].reshape(H * n, 256), WR[...]).reshape(H, n, C)
        m = jnp.where(inside[d0 : d0 + n][None], jnp.maximum(m, 0.0), 0.0)
        MF[:, d0 + 8 : d0 + 8 + n, :] = m
        done = upto

    def shifts(y, carry):
        for j in range(3):
            JM[y + 1, :, 128 * j : 128 * j + 128] = MF[y, 7 + j : 7 + j + D, :].astype(BF)
        return carry

    lax.fori_loop(0, H, shifts, 0)

    def joint(p, carry):
        h = dot(pairs(JM, 4 * p, 2), WM[...].reshape(1536, 256)) + HF[p]
        for u in range(2):
            for o in range(2):
                ho = h[D * u : D * u + D, 128 * o : 128 * o + 128]
                ho = jnp.where(inside, jnp.maximum(ho, 0.0), 0.0)
                for j in range(3):
                    sh = ho if j == 1 else pltpu.roll(ho, (2 - 2 * j) % D, 0)
                    H3[4 * p + 2 * u + o + 2, :, 128 * j : 128 * j + 128] = sh.astype(BF)
        return carry

    lax.fori_loop(0, H // 4, joint, 0)

    def dilated(p, carry):
        h = dot(pairs(H3, 4 * p, 1), W2[...].reshape(1536, 256))
        rows = []
        for yy in range(R):
            u, o = yy % 2, yy // 2
            ho = h[D * u : D * u + D, 128 * o : 128 * o + 128]
            ho = jnp.where(inside, jnp.maximum(ho, 0.0), 0.0)
            rows.append(
                jnp.concatenate([pltpu.roll(ho, (-7 - j) % D, 0)[:X].astype(BF) for j in range(3)], axis=1)
            )
        res = dot_t(W4[...].astype(BF), jnp.concatenate(rows, axis=0))
        for yy in range(R):
            RS[R * p + yy + 1] = res[:, X * yy : X * yy + X]
        return carry

    lax.fori_loop(0, NF, dilated, 0)

    def head(rr, carry):
        for yy in range(R):
            y = R * rr + yy
            res = RS[y, 0:2, :] + RS[y + 1, 2:4, :] + RS[y + 2, 4:6, :]
            OS[rr, :, yy : yy + 1, :] = res.reshape(2, 1, X)
        return carry

    lax.fori_loop(0, NF, head, 0)

    out_copies = []
    for o in range(1, nrow):
        there = lax.rem(row + o, nrow)
        cp = remote(OS.at[there], RO.at[row], osend.at[o - 1], orecv.at[o - 1], (tm, there, col))
        cp.start()
        out_copies.append(cp)
    RO[row] = OS[row]
    for cp in out_copies:
        cp.wait_recv()
    out[...] = RO[...]

    for cp in feat_copies + sum(msg_copies, []) + border_copies + out_copies:
        cp.wait_send()
    for side, has in ((0, has_left), (1, has_right)):

        @pl.when(has)
        def _(side=side):
            for cp in edge_copies(side):
                cp.wait_send()


def solution(mesh):
    ntm, ncol = mesh.shape["tm"], mesh.shape["col"]

    def step(feat, keys, kidx, mw, jw, dw, fw):
        anyspec = pl.BlockSpec(memory_space=pltpu.HBM)
        vspec = pl.BlockSpec(memory_space=pltpu.VMEM)
        dma = pltpu.SemaphoreType.DMA
        return pl.pallas_call(
            functools.partial(kernel, ntm, ncol),
            out_shape=jax.ShapeDtypeStruct((NF, 2, R, X), F32),
            in_specs=[
                pl.BlockSpec(memory_space=pltpu.SMEM),
                anyspec,
                anyspec,
                anyspec,
                anyspec,
                anyspec,
                anyspec,
            ],
            out_specs=vspec,
            scratch_shapes=[
                pltpu.VMEM((NF, R, X, C), BF),
                pltpu.VMEM((2, R, X, C), BF),
                pltpu.VMEM((R, X, C), BF),
                pltpu.VMEM((2, NF, R, 16, C), BF),
                pltpu.VMEM((2, R * 8, C), BF),
                pltpu.VMEM((2, NF, R * 8, C), BF),
                pltpu.VMEM((2, 2, R * 8, C), BF),
                pltpu.VMEM((2, NF, R * 8, C), BF),
                pltpu.VMEM((3, R, X, C), BF),
                pltpu.VMEM((NF, R, X, C), BF),
                pltpu.VMEM((3, 128, C), BF),
                pltpu.VMEM((NF, 128, C), BF),
                pltpu.VMEM((81, C), BF),
                pltpu.VMEM((2, 9 * C), BF),
                pltpu.VMEM((H, D, C), F32),
                pltpu.VMEM((H, E, C), F32),
                pltpu.VMEM((H, D, 256), BF),
                pltpu.VMEM((256, C), BF),
                pltpu.VMEM((H, D + 16, C), F32),
                pltpu.VMEM((H + 2, D, 384), BF),
                pltpu.VMEM((H + 2, D, 384), BF),
                pltpu.VMEM((4, 3, C, 256), BF),
                pltpu.VMEM((4, 3, C, 256), BF),
                pltpu.VMEM((H // 4, 2 * D, 256), F32),
                pltpu.VMEM((H + 4, D, 384), BF),
                pltpu.VMEM((4, 384, 256), BF),
                pltpu.VMEM((8, 384), F32),
                pltpu.VMEM((H + 2, 8, X), F32),
                pltpu.VMEM((NF, 2, R, X), F32),
                pltpu.VMEM((NF, 2, R, X), F32),
                dma((6,)),
                dma((3, 3, 2)),
                dma,
                dma,
                dma((2, 3)),
                dma((2, 3)),
                dma((3,)),
                dma((3,)),
                dma((NCH, 3)),
                dma((NCH, 3)),
                dma((3,)),
                dma((3,)),
                pltpu.SemaphoreType.REGULAR,
                dma((3,)),
                dma((3,)),
            ],
            compiler_params=pltpu.CompilerParams(
                collective_id=0, has_side_effects=True, vmem_limit_bytes=60 * 1024 * 1024
            ),
        )(
            kidx.reshape(NF),
            feat,
            keys,
            mw,
            jw,
            dw.reshape(3, 384, 128),
            fw.reshape(2, 1152),
        )

    in_specs = (
        P("tm", "row", "col", None),
        P("tm", "row", "col", None),
        P("tm", None),
        P(),
        P(),
        P(),
        P(),
    )
    return jax.shard_map(
        step, mesh=mesh, in_specs=in_specs, out_specs=P("tm", None, "row", "col"), check_vma=False
    )
```

```python
import functools
import math

import jax
import jax.numpy as jnp
from jax import lax
from jax.experimental import pallas as pl
from jax.experimental.pallas import tpu as pltpu
from jax.sharding import PartitionSpec as P

MESH = pl.DeviceIdType.MESH
BF = jnp.bfloat16
F32 = jnp.float32

NF = 4
R = 4
X = 128
C = 128
H = NF * R
D = X + 16
E = X + 32
NCH = 4
CH = X // NCH


def dot(a, b):
    return jnp.dot(a, b, preferred_element_type=F32)


def dot_t(a, b):
    return lax.dot_general(a, b, (((1,), (1,)), ((), ())), preferred_element_type=F32)


def kernel(
    ntm,
    ncol,
    kidx,
    feat,
    keys,
    mw,
    jw,
    dw,
    fw,
    out,
    F,
    KK,
    KV,
    FE,
    ES_K,
    ES_F,
    EKL,
    EKR,
    EF,
    SB,
    RB,
    SH,
    RH,
    MW,
    FW,
    FQ,
    KR,
    CB,
    WR,
    MF,
    JF,
    JM,
    WF,
    WM,
    HF,
    H3,
    W2,
    W4,
    HB,
    RS,
    OS,
    loc_sem,
    w_sem,
    ksend,
    krecv,
    esend,
    erecv,
    fsend,
    frecv,
    msend,
    mrecv,
    osend,
    orecv,
    ready,
    hsend,
    hrecv,
):
    EK = (EKL, EKR)
    tm = lax.axis_index("tm")
    row = lax.axis_index("row")
    col = lax.axis_index("col")
    nrow = NF
    tm_next = lax.rem(tm + 1, ntm)
    tm_prev = lax.rem(tm + ntm - 1, ntm)
    has_left = col > 0
    has_right = col < ncol - 1

    def local(src, dst, sem):
        cp = pltpu.make_async_copy(src, dst, sem)
        cp.start()
        return cp

    cross_left = has_left & (lax.rem(col, 2) == 0)
    cross_right = has_right & (lax.rem(col, 2) == 1)
    near_left = has_left & (lax.rem(col, 2) == 1)
    near_right = has_right & (lax.rem(col, 2) == 0)

    bar = pltpu.get_barrier_semaphore()

    def greet(t, r, c):
        pl.semaphore_signal(bar, inc=1, device_id=(t, r, c), device_id_type=MESH)

    for o in range(1, nrow):
        greet(tm, lax.rem(row + o, nrow), col)
    greet(tm_prev, row, col)

    @pl.when(cross_right)
    def _():
        greet(tm, row, col + 1)
        greet(tm_prev, row, col + 1)
        greet(tm_next, row, col + 1)

    @pl.when(near_left)
    def _():
        greet(tm, row, col - 1)
        greet(tm_prev, row, col - 1)

    @pl.when(near_right)
    def _():
        greet(tm, row, col + 1)
        greet(tm_prev, row, col + 1)

    own_key = local(keys.at[0], KV, loc_sem.at[0])
    edge_l = local(feat.at[:, :, pl.ds(0, 16), :], FE.at[0], loc_sem.at[1])
    edge_r = local(feat.at[:, :, pl.ds(X - 16, 16), :], FE.at[1], loc_sem.at[2])
    own_feat = local(feat.at[row], F.at[row], loc_sem.at[3])
    weights = [local(mw, MW, loc_sem.at[4]), local(fw, FW, loc_sem.at[5])]
    for i in range(3):
        for o in range(2):
            half = pl.ds(128 * o, 128)
            weights.append(local(jw.at[i, :, pl.ds(0, C), :], WM.at[i + o, :, :, half], w_sem.at[0, i, o]))
            weights.append(local(jw.at[i, :, pl.ds(C, C), :], WF.at[i + o, :, :, half], w_sem.at[1, i, o]))
            weights.append(local(dw.at[i], W2.at[i + o, :, half], w_sem.at[2, i, o]))

    own_key.wait()
    ri = lax.broadcasted_iota(jnp.int32, (X, X), 0)
    ci = lax.broadcasted_iota(jnp.int32, (X, X), 1)
    turn = (ri + ci == X - 1).astype(F32).astype(BF)
    for yy in range(R):
        KK[1, yy] = dot(turn, KV[yy]).astype(BF)

    edge_l.wait()
    edge_r.wait()
    for side in range(2):
        kv = KK[1, :, :16, :].astype(F32)[:, :8, :] if side else KK[1, :, X - 16 :, :].astype(F32)[:, 8:, :]
        ES_K[side] = kv.reshape(R * 8, C).astype(BF)
        for f in range(NF):
            fv = FE[side, f].astype(F32)[:, 8 * side : 8 * side + 8, :]
            ES_F[side, f] = fv.reshape(R * 8, C).astype(BF)

    one = lambda flag, n: n * flag.astype(jnp.int32)
    pl.semaphore_wait(bar, nrow + one(near_left, 2) + one(near_right, 2) + one(cross_left, 3))

    @pl.when(cross_left)
    def _():
        for t in (tm, tm_prev):
            pl.semaphore_signal(ready, inc=1, device_id=(t, row, col - 1), device_id_type=MESH)

    def remote(src, dst, s, r, dev):
        return pltpu.make_async_remote_copy(
            src_ref=src, dst_ref=dst, send_sem=s, recv_sem=r, device_id=dev, device_id_type=MESH
        )

    def edge_copies(side):
        other = 1 - side
        c = col + 2 * side - 1
        return [
            remote(ES_K.at[side], EK[other].at[0], esend.at[side, 0], erecv.at[other, 0], (tm_next, row, c)),
            remote(ES_K.at[side], EK[other].at[1], esend.at[side, 1], erecv.at[other, 1], (tm, row, c)),
            remote(ES_F.at[side], EF.at[other], esend.at[side, 2], erecv.at[other, 2], (tm, row, c)),
        ]

    def edge_waits(side):
        c = col + 2 * side - 1
        return [
            remote(ES_K.at[side], EK[side].at[0], esend.at[side, 0], erecv.at[side, 0], (tm_next, row, c)),
            remote(ES_K.at[side], EK[side].at[1], esend.at[side, 1], erecv.at[side, 1], (tm, row, c)),
            remote(ES_F.at[side], EF.at[side], esend.at[side, 2], erecv.at[side, 2], (tm, row, c)),
        ]

    for side, go in ((0, has_left), (1, near_right)):

        @pl.when(go)
        def _(side=side):
            for cp in edge_copies(side):
                cp.start()

    key_copy = remote(KK.at[1], KK.at[0], ksend, krecv, (tm_next, row, col))
    key_copy.start()
    feat_copies = []
    for o in (2, 1, 3):
        there = lax.rem(row + o, nrow)
        cp = remote(feat.at[there], F.at[row], fsend.at[o - 1], frecv.at[o - 1], (tm, there, col))
        cp.start()
        feat_copies.append(cp)

    for w in weights:
        w.wait()
    q = lax.broadcasted_iota(jnp.int32, (256, 81), 0)
    d = lax.broadcasted_iota(jnp.int32, (256, 81), 1)
    t = q & 15
    pick = (d == 9 * (q >> 4) + 15 - t) & (t >= 7) & (q < 144)
    WR[...] = dot(pick.astype(F32).astype(BF), MW[...]).astype(BF)

    zero = jnp.zeros((3, 128, 128), BF)
    for w in (WM, WF):
        w[0, :, :, 128:256] = zero
        w[3, :, :, 0:128] = zero
    W2[0, :, 128:256] = zero.reshape(384, 128)
    W2[3, :, 0:128] = zero.reshape(384, 128)
    W4[...] = jnp.zeros_like(W4)
    for j in range(3):
        for i in range(3):
            W4[8 * j + 2 * i : 8 * j + 2 * i + 2, :] = FW[:, 384 * i + 128 * j : 384 * i + 128 * j + 128].astype(F32)
    for i in (0, H + 1):
        JF[i] = jnp.zeros((D, 384), BF)
        JM[i] = jnp.zeros((D, 384), BF)
        RS[i] = jnp.zeros((8, X), F32)
    for i in (0, 1, H + 2, H + 3):
        H3[i] = jnp.zeros((D, 384), BF)
    KR[:, 0:8, :] = jnp.zeros((H, 8, C), F32)
    KR[:, E - 16 :, :] = jnp.zeros((H, 16, C), F32)
    MF[:, 0:8, :] = jnp.zeros((H, 8, C), F32)
    MF[:, D + 8 :, :] = jnp.zeros((H, 8, C), F32)

    dd = lax.broadcasted_iota(jnp.int32, (D, C), 0)
    inside = (has_left | (dd >= 8)) & (has_right | (dd < X + 8))

    slots = [
        jnp.where(kidx[lax.rem(row + o, nrow)] == tm, 1, 0) for o in range(nrow)
    ]

    def border_copies(side):
        return [
            remote(
                SH.at[side, o - 1],
                RH.at[row, side],
                hsend.at[side, o - 1],
                hrecv.at[side, o - 1],
                (tm, lax.rem(row + o, nrow), col),
            )
            for o in (2, 1, 3)
        ]

    def fill_border(dst, o, side):
        dst[0:32, :] = EK[side][slots[o]]
        dst[32:64, :] = EF[side, lax.rem(row + o, nrow)]

    def pass_border(side):
        for cp in edge_waits(side):
            cp.wait_recv()
        for o, cp in zip((2, 1, 3), border_copies(side)):
            fill_border(SH.at[side, o - 1], o, side)
            cp.start()
        fill_border(RH.at[row, side], 0, side)

    @pl.when(has_left)
    def _():
        pass_border(0)

    @pl.when(near_right)
    def _():
        pass_border(1)

    key_copy.wait()
    msg_copies = []
    for k in range(NCH):
        if k == NCH // 2:

            @pl.when(cross_right)
            def _():
                pl.semaphore_wait(ready, 2)
                for cp in edge_copies(1):
                    cp.start()
                pass_border(1)

        part = slice(X - (k + 1) * CH, X - k * CH)
        ds = pl.ds(X - (k + 1) * CH, CH)
        copies = []
        for o in (2, 1, 3):
            there = lax.rem(row + o, nrow)
            SB[o - 1, :, part, :] = KK[slots[o], :, part, :]
            cp = remote(
                SB.at[o - 1, :, ds, :], RB.at[row, :, ds, :], msend.at[k, o - 1], mrecv.at[k, o - 1], (tm, there, col)
            )
            cp.start()
            copies.append(cp)
        msg_copies.append(copies)
    RB[row] = KK[slots[0]]

    own_feat.wait()
    for cp in feat_copies:
        cp.wait_recv()
    for side, has in ((0, has_left), (1, has_right)):

        @pl.when(has)
        def _(side=side):
            for cp in border_copies(side):
                cp.wait_recv()


    def arrange(rs, carry):
        left = jnp.where(has_left, RH[rs, 0].astype(F32), 0.0)
        right = jnp.where(has_right, RH[rs, 1].astype(F32), 0.0)
        for yy in range(R):
            y = R * rs + yy
            b = 8 * yy
            KR[y, 140:148, :] = left[b : b + 8]
            KR[y, 4:12, :] = right[b : b + 8]
            fr = jnp.concatenate([left[32 + b : 40 + b], F[rs, yy].astype(F32), right[32 + b : 40 + b]], axis=0)
            FQ[y] = fr
            for j in range(3):
                sh = fr if j == 1 else pltpu.roll(fr, (1 - j) % D, 0)
                JF[y + 1, :, 128 * j : 128 * j + 128] = sh.astype(BF)
        return carry

    lax.fori_loop(0, NF, arrange, 0)

    def pairs(src, first, gap):
        return jnp.concatenate(
            [
                jnp.concatenate([src[first + t * (3 - gap)] for t in range(4)], axis=1),
                jnp.concatenate([src[first + gap + t * (3 - gap)] for t in range(4)], axis=1),
            ],
            axis=0,
        )

    def joint_frames(p, carry):
        HF[p] = dot(pairs(JF, 4 * p, 2), WF[...].reshape(1536, 256))
        return carry

    lax.fori_loop(0, H // 4, joint_frames, 0)

    scale = 1.0 / math.sqrt(C)
    lane = lax.broadcasted_iota(jnp.int32, (8, 128), 1)

    def correlate(p, carry):
        parts = [[], []]
        for h in range(2):
            d0 = pl.multiple_of(16 * p + 8 * h, 8)
            e0 = pl.multiple_of(136 - 16 * p - 8 * h, 8)
            qs = FQ[:, pl.ds(d0, 8), :].reshape(H * 8, C).astype(BF)
            ks = KR[:, pl.ds(e0, 16), :].reshape(H * 16, C).astype(BF)
            sc = (dot_t(qs, ks) * scale).reshape(H, 8, 256)
            for y in range(H):
                turn = (64 - 16 * y) % 256
                by = turn % 128
                lo = pltpu.roll(sc[y, :, :128], by, 1, stride=1, stride_axis=0)
                hi = pltpu.roll(sc[y, :, 128:], by, 1, stride=1, stride_axis=0)
                if turn >= 128:
                    lo, hi = hi, lo
                low = jnp.where(lane < by, hi, lo) if by else lo
                high = jnp.where(lane < by, lo, hi) if by else hi
                if y < 4:
                    low = jnp.where(lane >= 16 * (4 - y), low, 0.0)
                if y > 11:
                    high = jnp.zeros_like(high)
                if y > 12:
                    low = jnp.where(lane < 16 * (20 - y), low, 0.0)
                parts[h].append(jnp.concatenate([low, high], axis=1))
        c0 = pl.multiple_of(16 * p, 16)
        for y in range(H):
            CB[y, pl.ds(c0, 16), :] = jnp.concatenate([parts[0][y], parts[1][y]], axis=0).astype(BF)
        return carry

    done = 0
    shifted = 0
    for k in range(NCH):
        for cp in msg_copies[k]:
            cp.wait_recv()
        s0 = X - (k + 1) * CH

        def place(rs, carry, s0=s0):
            y0 = R * rs
            for yy in range(R):
                KR[y0 + yy, 12 + s0 : 12 + s0 + CH, :] = RB[rs, yy, s0 : s0 + CH, :].astype(F32)
            return carry

        lax.fori_loop(0, NF, place, 0)
        upto = D // 16 if k == NCH - 1 else ((k + 1) * CH - 12) // 16 + 1
        lax.fori_loop(done, upto, correlate, 0)
        n = 16 * (upto - done)
        d0 = 16 * done
        m = dot(CB[:, d0 : d0 + n, :].reshape(H * n, 256), WR[...]).reshape(H, n, C)
        m = jnp.where(inside[d0 : d0 + n][None], jnp.maximum(m, 0.0), 0.0)
        MF[:, d0 + 8 : d0 + 8 + n, :] = m
        done = upto
        d1 = D if k == NCH - 1 else 16 * done - 16

        def shifts(y, carry, d0=shifted, d1=d1):
            for j in range(3):
                JM[y + 1, d0:d1, 128 * j : 128 * j + 128] = MF[y, 7 + j + d0 : 7 + j + d1, :].astype(BF)
            return carry

        lax.fori_loop(0, H, shifts, 0)
        shifted = d1

    def joint(p, carry):
        h = dot(pairs(JM, 4 * p, 2), WM[...].reshape(1536, 256)) + HF[p]
        for u in range(2):
            for o in range(2):
                ho = h[D * u : D * u + D, 128 * o : 128 * o + 128]
                ho = jnp.where(inside, jnp.maximum(ho, 0.0), 0.0)
                for j in range(3):
                    sh = ho if j == 1 else pltpu.roll(ho, (2 - 2 * j) % D, 0)
                    H3[4 * p + 2 * u + o + 2, :, 128 * j : 128 * j + 128] = sh.astype(BF)
        return carry

    lax.fori_loop(0, H // 4, joint, 0, unroll=True)

    def dilated(p, carry):
        h = dot(pairs(H3, 4 * p, 1), W2[...].reshape(1536, 256))
        for yy in range(R):
            u, o = yy % 2, yy // 2
            ho = h[D * u : D * u + D, 128 * o : 128 * o + 128]
            HB[R * p + yy] = jnp.where(inside, jnp.maximum(ho, 0.0), 0.0).astype(BF)
        return carry

    lax.fori_loop(0, NF, dilated, 0, unroll=True)

    def taps(p, carry):
        res = dot_t(W4[...].astype(BF), HB[pl.ds(R * p, R)].reshape(R * D, C))
        for yy in range(R):
            RS[R * p + yy + 1] = sum(
                res[8 * j : 8 * j + 8, D * yy + 7 + j : D * yy + 7 + j + X] for j in range(3)
            )
        return carry

    lax.fori_loop(0, NF, taps, 0, unroll=True)

    def head(rr, carry):
        for yy in range(R):
            y = R * rr + yy
            res = RS[y, 0:2, :] + RS[y + 1, 2:4, :] + RS[y + 2, 4:6, :]
            OS[rr, :, yy : yy + 1, :] = res.reshape(2, 1, X)
        return carry

    lax.fori_loop(0, NF, head, 0, unroll=True)

    out_copies = []
    for o in range(1, nrow):
        there = lax.rem(row + o, nrow)
        cp = remote(OS.at[there], out.at[row], osend.at[o - 1], orecv.at[o - 1], (tm, there, col))
        cp.start()
        out_copies.append(cp)
    own_out = local(OS.at[row], out.at[row], loc_sem.at[6])
    own_out.wait()
    for cp in out_copies:
        cp.wait_recv()

    for cp in feat_copies + sum(msg_copies, []) + out_copies:
        cp.wait_send()
    for side, has in ((0, has_left), (1, has_right)):

        @pl.when(has)
        def _(side=side):
            for cp in edge_copies(side) + border_copies(side):
                cp.wait_send()


def solution(mesh):
    ntm, ncol = mesh.shape["tm"], mesh.shape["col"]

    def step(feat, keys, kidx, mw, jw, dw, fw):
        anyspec = pl.BlockSpec(memory_space=pltpu.HBM)
        dma = pltpu.SemaphoreType.DMA
        return pl.pallas_call(
            functools.partial(kernel, ntm, ncol),
            out_shape=jax.ShapeDtypeStruct((NF, 2, R, X), F32),
            in_specs=[
                pl.BlockSpec(memory_space=pltpu.SMEM),
                anyspec,
                anyspec,
                anyspec,
                anyspec,
                anyspec,
                anyspec,
            ],
            out_specs=anyspec,
            scratch_shapes=[
                pltpu.VMEM((NF, R, X, C), BF),
                pltpu.VMEM((2, R, X, C), BF),
                pltpu.VMEM((R, X, C), BF),
                pltpu.VMEM((2, NF, R, 16, C), BF),
                pltpu.VMEM((2, R * 8, C), BF),
                pltpu.VMEM((2, NF, R * 8, C), BF),
                pltpu.VMEM((2, R * 8, C), BF),
                pltpu.VMEM((2, R * 8, C), BF),
                pltpu.VMEM((2, NF, R * 8, C), BF),
                pltpu.VMEM((3, R, X, C), BF),
                pltpu.VMEM((NF, R, X, C), BF),
                pltpu.VMEM((2, 3, 64, C), BF),
                pltpu.VMEM((NF, 2, 64, C), BF),
                pltpu.VMEM((81, C), BF),
                pltpu.VMEM((2, 9 * C), BF),
                pltpu.VMEM((H, D, C), F32),
                pltpu.VMEM((H, E, C), F32),
                pltpu.VMEM((H, D, 256), BF),
                pltpu.VMEM((256, C), BF),
                pltpu.VMEM((H, D + 16, C), F32),
                pltpu.VMEM((H + 2, D, 384), BF),
                pltpu.VMEM((H + 2, D, 384), BF),
                pltpu.VMEM((4, 3, C, 256), BF),
                pltpu.VMEM((4, 3, C, 256), BF),
                pltpu.VMEM((H // 4, 2 * D, 256), F32),
                pltpu.VMEM((H + 4, D, 384), BF),
                pltpu.VMEM((4, 384, 256), BF),
                pltpu.VMEM((24, C), F32),
                pltpu.VMEM((H, D, C), BF),
                pltpu.VMEM((H + 2, 8, X), F32),
                pltpu.VMEM((NF, 2, R, X), F32),
                dma((7,)),
                dma((3, 3, 2)),
                dma,
                dma,
                dma((2, 3)),
                dma((2, 3)),
                dma((3,)),
                dma((3,)),
                dma((NCH, 3)),
                dma((NCH, 3)),
                dma((3,)),
                dma((3,)),
                pltpu.SemaphoreType.REGULAR,
                dma((2, 3)),
                dma((2, 3)),
            ],
            compiler_params=pltpu.CompilerParams(
                collective_id=0, has_side_effects=True, vmem_limit_bytes=60 * 1024 * 1024
            ),
        )(
            kidx.reshape(NF),
            feat,
            keys,
            mw,
            jw,
            dw.reshape(3, 384, 128),
            fw.reshape(2, 1152),
        )

    in_specs = (
        P("tm", "row", "col", None),
        P("tm", "row", "col", None),
        P("tm", None),
        P(),
        P(),
        P(),
        P(),
    )
    return jax.shard_map(
        step, mesh=mesh, in_specs=in_specs, out_specs=P("tm", None, "row", "col"), check_vma=False
    )
```

```python
import functools
import math

import jax
import jax.numpy as jnp
from jax import lax
from jax.experimental import pallas as pl
from jax.experimental.pallas import tpu as pltpu
from jax.sharding import PartitionSpec as P

MESH = pl.DeviceIdType.MESH
BF = jnp.bfloat16
F32 = jnp.float32

NF = 4
R = 4
X = 128
C = 128
H = NF * R
D = X + 16
E = X + 32
NCH = 4
CH = X // NCH


def dot(a, b):
    return jnp.dot(a, b, preferred_element_type=F32)


def dot_t(a, b):
    return lax.dot_general(a, b, (((1,), (1,)), ((), ())), preferred_element_type=F32)


def kernel(
    ntm,
    ncol,
    kidx,
    feat,
    keys,
    mw,
    jw,
    dw,
    fw,
    out,
    F,
    KK,
    KV,
    FE,
    ES_K,
    ES_F,
    EKL,
    EKR,
    EF,
    SB,
    RB,
    SH,
    RH,
    MW,
    FW,
    FQ,
    KR,
    CB,
    WR,
    MF,
    JF,
    JM,
    WF,
    WM,
    HF,
    H3,
    W2,
    W4,
    HB,
    RS,
    OS,
    loc_sem,
    w_sem,
    ksend,
    krecv,
    esend,
    erecv,
    fsend,
    frecv,
    msend,
    mrecv,
    osend,
    orecv,
    ready,
    hsend,
    hrecv,
):
    EK = (EKL, EKR)
    tm = lax.axis_index("tm")
    row = lax.axis_index("row")
    col = lax.axis_index("col")
    nrow = NF
    tm_next = lax.rem(tm + 1, ntm)
    tm_prev = lax.rem(tm + ntm - 1, ntm)
    has_next = tm < ntm - 1
    has_prev = tm > 0
    has_left = col > 0
    has_right = col < ncol - 1

    def local(src, dst, sem):
        cp = pltpu.make_async_copy(src, dst, sem)
        cp.start()
        return cp

    cross_left = has_left & (lax.rem(col, 2) == 0)
    cross_right = has_right & (lax.rem(col, 2) == 1)
    near_left = has_left & (lax.rem(col, 2) == 1)
    near_right = has_right & (lax.rem(col, 2) == 0)

    bar = pltpu.get_barrier_semaphore()

    def greet(t, r, c):
        pl.semaphore_signal(bar, inc=1, device_id=(t, r, c), device_id_type=MESH)

    for o in range(1, nrow):
        greet(tm, lax.rem(row + o, nrow), col)
    greet(tm_prev, row, col)

    @pl.when(cross_right)
    def _():
        greet(tm, row, col + 1)
        greet(tm_prev, row, col + 1)
        greet(tm_next, row, col + 1)

    @pl.when(near_left)
    def _():
        greet(tm, row, col - 1)
        greet(tm_prev, row, col - 1)

    @pl.when(near_right)
    def _():
        greet(tm, row, col + 1)
        greet(tm_prev, row, col + 1)

    own_key = local(keys.at[0], KV, loc_sem.at[0])
    edge_l = local(feat.at[:, :, pl.ds(0, 16), :], FE.at[0], loc_sem.at[1])
    edge_r = local(feat.at[:, :, pl.ds(X - 16, 16), :], FE.at[1], loc_sem.at[2])
    own_feat = local(feat.at[row], F.at[row], loc_sem.at[3])
    weights = [local(mw, MW, loc_sem.at[4]), local(fw, FW, loc_sem.at[5])]
    for i in range(3):
        for o in range(2):
            half = pl.ds(128 * o, 128)
            weights.append(local(jw.at[i, :, pl.ds(0, C), :], WM.at[i + o, :, :, half], w_sem.at[0, i, o]))
            weights.append(local(jw.at[i, :, pl.ds(C, C), :], WF.at[i + o, :, :, half], w_sem.at[1, i, o]))
            weights.append(local(dw.at[i], W2.at[i + o, :, half], w_sem.at[2, i, o]))

    own_key.wait()
    ri = lax.broadcasted_iota(jnp.int32, (X, X), 0)
    ci = lax.broadcasted_iota(jnp.int32, (X, X), 1)
    turn = (ri + ci == X - 1).astype(F32).astype(BF)
    for yy in range(R):
        KK[1, yy] = dot(turn, KV[yy]).astype(BF)

    edge_l.wait()
    edge_r.wait()
    for side in range(2):
        kv = KK[1, :, :16, :].astype(F32)[:, :8, :] if side else KK[1, :, X - 16 :, :].astype(F32)[:, 8:, :]
        ES_K[side] = kv.reshape(R * 8, C).astype(BF)
        for f in range(NF):
            fv = FE[side, f].astype(F32)[:, 8 * side : 8 * side + 8, :]
            ES_F[side, f] = fv.reshape(R * 8, C).astype(BF)

    one = lambda flag, n: n * flag.astype(jnp.int32)
    pl.semaphore_wait(bar, nrow + one(near_left, 2) + one(near_right, 2) + one(cross_left, 3))

    @pl.when(cross_left)
    def _():
        for t in (tm, tm_prev):
            pl.semaphore_signal(ready, inc=1, device_id=(t, row, col - 1), device_id_type=MESH)

    def remote(src, dst, s, r, dev):
        return pltpu.make_async_remote_copy(
            src_ref=src, dst_ref=dst, send_sem=s, recv_sem=r, device_id=dev, device_id_type=MESH
        )

    def edge_copies(side):
        other = 1 - side
        c = col + 2 * side - 1
        return [
            remote(ES_K.at[side], EK[other].at[0], esend.at[side, 0], erecv.at[other, 0], (tm_next, row, c)),
            remote(ES_K.at[side], EK[other].at[1], esend.at[side, 1], erecv.at[other, 1], (tm, row, c)),
            remote(ES_F.at[side], EF.at[other], esend.at[side, 2], erecv.at[other, 2], (tm, row, c)),
        ]

    def edge_waits(side):
        c = col + 2 * side - 1
        return [
            remote(ES_K.at[side], EK[side].at[0], esend.at[side, 0], erecv.at[side, 0], (tm_next, row, c)),
            remote(ES_K.at[side], EK[side].at[1], esend.at[side, 1], erecv.at[side, 1], (tm, row, c)),
            remote(ES_F.at[side], EF.at[side], esend.at[side, 2], erecv.at[side, 2], (tm, row, c)),
        ]

    def start_edges(side):
        to_next, *others = edge_copies(side)
        for cp in others:
            cp.start()

        @pl.when(has_next)
        def _():
            to_next.start()

    for side, go in ((0, has_left), (1, near_right)):

        @pl.when(go)
        def _(side=side):
            start_edges(side)

    key_copy = remote(KK.at[1], KK.at[0], ksend, krecv, (tm_next, row, col))

    @pl.when(has_next)
    def _():
        key_copy.start()

    feat_copies = []
    for o in (2, 1, 3):
        there = lax.rem(row + o, nrow)
        cp = remote(feat.at[there], F.at[row], fsend.at[o - 1], frecv.at[o - 1], (tm, there, col))
        cp.start()
        feat_copies.append(cp)

    for w in weights:
        w.wait()
    q = lax.broadcasted_iota(jnp.int32, (256, 81), 0)
    d = lax.broadcasted_iota(jnp.int32, (256, 81), 1)
    t = q & 15
    pick = (d == 9 * (q >> 4) + 15 - t) & (t >= 7) & (q < 144)
    WR[...] = dot(pick.astype(F32).astype(BF), MW[...]).astype(BF)

    zero = jnp.zeros((3, 128, 128), BF)
    for w in (WM, WF):
        w[0, :, :, 128:256] = zero
        w[3, :, :, 0:128] = zero
    W2[0, :, 128:256] = zero.reshape(384, 128)
    W2[3, :, 0:128] = zero.reshape(384, 128)
    W4[...] = jnp.zeros_like(W4)
    for j in range(3):
        for i in range(3):
            W4[8 * j + 2 * i : 8 * j + 2 * i + 2, :] = FW[:, 384 * i + 128 * j : 384 * i + 128 * j + 128].astype(F32)
    for i in (0, H + 1):
        JF[i] = jnp.zeros((D, 384), BF)
        JM[i] = jnp.zeros((D, 384), BF)
        RS[i] = jnp.zeros((8, X), F32)
    for i in (0, 1, H + 2, H + 3):
        H3[i] = jnp.zeros((D, 384), BF)
    KR[:, 0:8, :] = jnp.zeros((H, 8, C), F32)
    KR[:, E - 16 :, :] = jnp.zeros((H, 16, C), F32)
    MF[:, 0:8, :] = jnp.zeros((H, 8, C), F32)
    MF[:, D + 8 :, :] = jnp.zeros((H, 8, C), F32)

    dd = lax.broadcasted_iota(jnp.int32, (D, C), 0)
    inside = (has_left | (dd >= 8)) & (has_right | (dd < X + 8))

    slots = [
        jnp.where(kidx[lax.rem(row + o, nrow)] == tm, 1, 0) for o in range(nrow)
    ]

    def border_copies(side):
        return [
            remote(
                SH.at[side, o - 1],
                RH.at[row, side],
                hsend.at[side, o - 1],
                hrecv.at[side, o - 1],
                (tm, lax.rem(row + o, nrow), col),
            )
            for o in (2, 1, 3)
        ]

    def fill_border(dst, o, side):
        dst[0:32, :] = EK[side][slots[o]]
        dst[32:64, :] = EF[side, lax.rem(row + o, nrow)]

    def pass_border(side):
        from_prev, *others = edge_waits(side)
        for cp in others:
            cp.wait_recv()

        @pl.when(has_prev)
        def _():
            from_prev.wait_recv()

        for o, cp in zip((2, 1, 3), border_copies(side)):
            fill_border(SH.at[side, o - 1], o, side)
            cp.start()
        fill_border(RH.at[row, side], 0, side)

    @pl.when(near_left)
    def _():
        pass_border(0)

    @pl.when(near_right)
    def _():
        pass_border(1)


    @pl.when(has_next)
    def _():
        key_copy.wait_send()

    @pl.when(has_prev)
    def _():
        key_copy.wait_recv()

    msg_copies = []
    for k in range(NCH):
        if k == 1:

            @pl.when(cross_left)
            def _():
                pass_border(0)

        if k == 2:

            @pl.when(cross_right)
            def _():
                pl.semaphore_wait(ready, 2)
                start_edges(1)

        if k == 3:

            @pl.when(cross_right)
            def _():
                pass_border(1)

        part = slice(X - (k + 1) * CH, X - k * CH)
        ds = pl.ds(X - (k + 1) * CH, CH)
        copies = []
        for o in (2, 1, 3):
            there = lax.rem(row + o, nrow)
            SB[o - 1, :, part, :] = KK[slots[o], :, part, :]
            cp = remote(
                SB.at[o - 1, :, ds, :], RB.at[row, :, ds, :], msend.at[k, o - 1], mrecv.at[k, o - 1], (tm, there, col)
            )
            cp.start()
            copies.append(cp)
        msg_copies.append(copies)
    RB[row] = KK[slots[0]]

    own_feat.wait()
    for cp in feat_copies:
        cp.wait_recv()
    edge = jnp.zeros((8, C), F32)

    def arrange(rs, carry):
        for yy in range(R):
            y = R * rs + yy
            fr = jnp.concatenate([edge, F[rs, yy].astype(F32), edge], axis=0)
            FQ[y] = fr
            for j in range(3):
                sh = fr if j == 1 else pltpu.roll(fr, (1 - j) % D, 0)
                JF[y + 1, :, 128 * j : 128 * j + 128] = sh.astype(BF)
        return carry

    lax.fori_loop(0, NF, arrange, 0)

    def pairs(src, first, gap):
        return jnp.concatenate(
            [
                jnp.concatenate([src[first + t * (3 - gap)] for t in range(4)], axis=1),
                jnp.concatenate([src[first + gap + t * (3 - gap)] for t in range(4)], axis=1),
            ],
            axis=0,
        )

    def joint_frames(p, carry):
        HF[p] = dot(pairs(JF, 4 * p, 2), WF[...].reshape(1536, 256))
        return carry

    lax.fori_loop(0, H // 4, joint_frames, 0)

    scale = 1.0 / math.sqrt(C)
    lane = lax.broadcasted_iota(jnp.int32, (8, 128), 1)

    def correlate(p, carry):
        parts = [[], []]
        for h in range(2):
            d0 = pl.multiple_of(16 * p + 8 * h, 8)
            e0 = pl.multiple_of(136 - 16 * p - 8 * h, 8)
            qs = FQ[:, pl.ds(d0, 8), :].reshape(H * 8, C).astype(BF)
            ks = KR[:, pl.ds(e0, 16), :].reshape(H * 16, C).astype(BF)
            sc = (dot_t(qs, ks) * scale).reshape(H, 8, 256)
            for y in range(H):
                turn = (64 - 16 * y) % 256
                by = turn % 128
                lo = pltpu.roll(sc[y, :, :128], by, 1, stride=1, stride_axis=0)
                hi = pltpu.roll(sc[y, :, 128:], by, 1, stride=1, stride_axis=0)
                if turn >= 128:
                    lo, hi = hi, lo
                low = jnp.where(lane < by, hi, lo) if by else lo
                high = jnp.where(lane < by, lo, hi) if by else hi
                if y < 4:
                    low = jnp.where(lane >= 16 * (4 - y), low, 0.0)
                if y > 11:
                    high = jnp.zeros_like(high)
                if y > 12:
                    low = jnp.where(lane < 16 * (20 - y), low, 0.0)
                parts[h].append(jnp.concatenate([low, high], axis=1))
        c0 = pl.multiple_of(16 * p, 16)
        for y in range(H):
            CB[y, pl.ds(c0, 16), :] = jnp.concatenate([parts[0][y], parts[1][y]], axis=0).astype(BF)
        return carry

    def motion(corr, keep):
        n = corr.shape[1]
        m = dot(corr.reshape(H * n, 256), WR[...]).reshape(H, n, C)
        return jnp.where(keep[None], jnp.maximum(m, 0.0), 0.0)

    def shift(d0, d1):
        def shifts(y, carry):
            for j in range(3):
                JM[y + 1, d0:d1, 128 * j : 128 * j + 128] = MF[y, 7 + j + d0 : 7 + j + d1, :].astype(BF)
            return carry

        lax.fori_loop(0, H, shifts, 0)

    def amend(rs, carry):
        left = jnp.where(has_left, RH[rs, 0].astype(F32), 0.0)
        right = jnp.where(has_right, RH[rs, 1].astype(F32), 0.0)
        for yy in range(R):
            y = R * rs + yy
            b = 8 * yy
            KR[y, 140:148, :] = left[b : b + 8]
            KR[y, 4:12, :] = right[b : b + 8]
            lf, rf = left[32 + b : 40 + b], right[32 + b : 40 + b]
            FQ[y, 0:8, :] = lf
            FQ[y, D - 8 : D, :] = rf
            ends = (
                jnp.concatenate([lf, F[rs, yy, 0:16, :].astype(F32)], axis=0),
                jnp.concatenate([F[rs, yy, X - 16 :, :].astype(F32), rf], axis=0),
            )
            for side, at in ((0, 0), (1, D - 16)):
                for j in range(3):
                    sh = ends[side] if j == 1 else pltpu.roll(ends[side], (1 - j) % 24, 0)
                    JF[y + 1, at : at + 16, 128 * j : 128 * j + 128] = sh[8 * side : 8 * side + 16].astype(BF)
        return carry

    done = 1
    shifted = 32
    for k in range(NCH):
        if k == NCH - 1:
            for side, has in ((0, has_left), (1, has_right)):

                @pl.when(has)
                def _(side=side):
                    for cp in border_copies(side):
                        cp.wait_recv()

            lax.fori_loop(0, NF, amend, 0)

            spots = [(p, u, at) for p in range(H // 4) for u in range(2) for at in (0, D - 16)]
            lhs = jnp.concatenate(
                [
                    jnp.concatenate([JF[4 * p + 2 * u + t, at : at + 16, :] for t in range(4)], axis=1)
                    for p, u, at in spots
                ],
                axis=0,
            )
            hf = dot(lhs, WF[...].reshape(1536, 256))
            for i, (p, u, at) in enumerate(spots):
                HF[p, D * u + at : D * u + at + 16, :] = hf[16 * i : 16 * i + 16]

            correlate(0, 0)
            MF[:, 8:24, :] = motion(CB[:, 0:16, :], inside[0:16])
            shift(0, 32)

        for cp in msg_copies[k]:
            cp.wait_recv()
        s0 = X - (k + 1) * CH

        def place(rs, carry, s0=s0):
            y0 = R * rs
            for yy in range(R):
                KR[y0 + yy, 12 + s0 : 12 + s0 + CH, :] = RB[rs, yy, s0 : s0 + CH, :].astype(F32)
            return carry

        lax.fori_loop(0, NF, place, 0)
        upto = D // 16 if k == NCH - 1 else ((k + 1) * CH - 12) // 16 + 1
        lax.fori_loop(done, upto, correlate, 0)
        d0, d1 = 16 * done, 16 * upto
        MF[:, d0 + 8 : d1 + 8, :] = motion(CB[:, d0:d1, :], inside[d0:d1])
        done = upto
        d1 = D if k == NCH - 1 else d1 - 16
        if d1 > shifted:
            shift(shifted, d1)
            shifted = d1

    def joint(p, carry):
        h = dot(pairs(JM, 4 * p, 2), WM[...].reshape(1536, 256)) + HF[p]
        for u in range(2):
            for o in range(2):
                ho = h[D * u : D * u + D, 128 * o : 128 * o + 128]
                ho = jnp.where(inside, jnp.maximum(ho, 0.0), 0.0)
                for j in range(3):
                    sh = ho if j == 1 else pltpu.roll(ho, (2 - 2 * j) % D, 0)
                    H3[4 * p + 2 * u + o + 2, :, 128 * j : 128 * j + 128] = sh.astype(BF)
        return carry

    lax.fori_loop(0, H // 4, joint, 0, unroll=True)

    def dilated(p, carry):
        h = dot(pairs(H3, 4 * p, 1), W2[...].reshape(1536, 256))
        for yy in range(R):
            u, o = yy % 2, yy // 2
            ho = h[D * u : D * u + D, 128 * o : 128 * o + 128]
            HB[R * p + yy] = jnp.where(inside, jnp.maximum(ho, 0.0), 0.0).astype(BF)
        return carry

    lax.fori_loop(0, NF, dilated, 0, unroll=True)

    def taps(p, carry):
        res = dot_t(W4[...].astype(BF), HB[pl.ds(R * p, R)].reshape(R * D, C))
        for yy in range(R):
            RS[R * p + yy + 1] = sum(
                res[8 * j : 8 * j + 8, D * yy + 7 + j : D * yy + 7 + j + X] for j in range(3)
            )
        return carry

    lax.fori_loop(0, NF, taps, 0, unroll=True)

    def head(rr, carry):
        for yy in range(R):
            y = R * rr + yy
            res = RS[y, 0:2, :] + RS[y + 1, 2:4, :] + RS[y + 2, 4:6, :]
            OS[rr, :, yy : yy + 1, :] = res.reshape(2, 1, X)
        return carry

    lax.fori_loop(0, NF, head, 0, unroll=True)

    out_copies = []
    for o in range(1, nrow):
        there = lax.rem(row + o, nrow)
        cp = remote(OS.at[there], out.at[row], osend.at[o - 1], orecv.at[o - 1], (tm, there, col))
        cp.start()
        out_copies.append(cp)
    own_out = local(OS.at[row], out.at[row], loc_sem.at[6])
    own_out.wait()
    for cp in out_copies:
        cp.wait_recv()

    for cp in feat_copies + sum(msg_copies, []) + out_copies:
        cp.wait_send()
    for side, has in ((0, has_left), (1, has_right)):

        @pl.when(has)
        def _(side=side):
            to_next, *others = edge_copies(side)
            for cp in others + border_copies(side):
                cp.wait_send()

            @pl.when(has_next)
            def _():
                to_next.wait_send()


def solution(mesh):
    ntm, ncol = mesh.shape["tm"], mesh.shape["col"]

    def step(feat, keys, kidx, mw, jw, dw, fw):
        anyspec = pl.BlockSpec(memory_space=pltpu.HBM)
        dma = pltpu.SemaphoreType.DMA
        return pl.pallas_call(
            functools.partial(kernel, ntm, ncol),
            out_shape=jax.ShapeDtypeStruct((NF, 2, R, X), F32),
            in_specs=[
                pl.BlockSpec(memory_space=pltpu.SMEM),
                anyspec,
                anyspec,
                anyspec,
                anyspec,
                anyspec,
                anyspec,
            ],
            out_specs=anyspec,
            scratch_shapes=[
                pltpu.VMEM((NF, R, X, C), BF),
                pltpu.VMEM((2, R, X, C), BF),
                pltpu.VMEM((R, X, C), BF),
                pltpu.VMEM((2, NF, R, 16, C), BF),
                pltpu.VMEM((2, R * 8, C), BF),
                pltpu.VMEM((2, NF, R * 8, C), BF),
                pltpu.VMEM((2, R * 8, C), BF),
                pltpu.VMEM((2, R * 8, C), BF),
                pltpu.VMEM((2, NF, R * 8, C), BF),
                pltpu.VMEM((3, R, X, C), BF),
                pltpu.VMEM((NF, R, X, C), BF),
                pltpu.VMEM((2, 3, 64, C), BF),
                pltpu.VMEM((NF, 2, 64, C), BF),
                pltpu.VMEM((81, C), BF),
                pltpu.VMEM((2, 9 * C), BF),
                pltpu.VMEM((H, D, C), F32),
                pltpu.VMEM((H, E, C), F32),
                pltpu.VMEM((H, D, 256), BF),
                pltpu.VMEM((256, C), BF),
                pltpu.VMEM((H, D + 16, C), F32),
                pltpu.VMEM((H + 2, D, 384), BF),
                pltpu.VMEM((H + 2, D, 384), BF),
                pltpu.VMEM((4, 3, C, 256), BF),
                pltpu.VMEM((4, 3, C, 256), BF),
                pltpu.VMEM((H // 4, 2 * D, 256), F32),
                pltpu.VMEM((H + 4, D, 384), BF),
                pltpu.VMEM((4, 384, 256), BF),
                pltpu.VMEM((24, C), F32),
                pltpu.VMEM((H, D, C), BF),
                pltpu.VMEM((H + 2, 8, X), F32),
                pltpu.VMEM((NF, 2, R, X), F32),
                dma((7,)),
                dma((3, 3, 2)),
                dma,
                dma,
                dma((2, 3)),
                dma((2, 3)),
                dma((3,)),
                dma((3,)),
                dma((NCH, 3)),
                dma((NCH, 3)),
                dma((3,)),
                dma((3,)),
                pltpu.SemaphoreType.REGULAR,
                dma((2, 3)),
                dma((2, 3)),
            ],
            compiler_params=pltpu.CompilerParams(
                collective_id=0, has_side_effects=True, vmem_limit_bytes=60 * 1024 * 1024
            ),
        )(
            kidx.reshape(NF),
            feat,
            keys,
            mw,
            jw,
            dw.reshape(3, 384, 128),
            fw.reshape(2, 1152),
        )

    in_specs = (
        P("tm", "row", "col", None),
        P("tm", "row", "col", None),
        P("tm", None),
        P(),
        P(),
        P(),
        P(),
    )
    return jax.shard_map(
        step, mesh=mesh, in_specs=in_specs, out_specs=P("tm", None, "row", "col"), check_vma=False
    )
```

```python
import functools
import math

import jax
import jax.numpy as jnp
from jax import lax
from jax.experimental import pallas as pl
from jax.experimental.pallas import tpu as pltpu
from jax.sharding import PartitionSpec as P

MESH = pl.DeviceIdType.MESH
BF = jnp.bfloat16
F32 = jnp.float32

NF = 4
R = 4
X = 128
C = 128
H = NF * R
D = X + 16
E = X + 32
PLAN = (((0, 1, 2), (0, 1)), ((3,), (2, 3)))
NCH = 4
CH = X // NCH


def dot(a, b):
    return jnp.dot(a, b, preferred_element_type=F32)


def dot_t(a, b):
    return lax.dot_general(a, b, (((1,), (1,)), ((), ())), preferred_element_type=F32)


def kernel(
    ntm,
    ncol,
    kidx,
    feat,
    keys,
    mw,
    jw,
    dw,
    fw,
    out,
    F,
    KK,
    KV,
    FE,
    ES_K,
    ES_F,
    EKL,
    EKR,
    EF,
    SB,
    RB,
    SH,
    RH,
    MW,
    FW,
    FQ,
    KR,
    CB,
    WR,
    MF,
    JF,
    JM,
    WF,
    WM,
    HF,
    H3,
    W2,
    W4,
    HB,
    RS,
    OS,
    loc_sem,
    w_sem,
    ksend,
    krecv,
    esend,
    erecv,
    fsend,
    frecv,
    msend,
    mrecv,
    osend,
    orecv,
    ready,
    hsend,
    hrecv,
):
    EK = (EKL, EKR)
    tm = lax.axis_index("tm")
    row = lax.axis_index("row")
    col = lax.axis_index("col")
    nrow = NF
    tm_next = lax.rem(tm + 1, ntm)
    tm_prev = lax.rem(tm + ntm - 1, ntm)
    has_next = tm < ntm - 1
    has_prev = tm > 0
    has_left = col > 0
    has_right = col < ncol - 1

    def local(src, dst, sem):
        cp = pltpu.make_async_copy(src, dst, sem)
        cp.start()
        return cp

    cross_left = has_left & (lax.rem(col, 2) == 0)
    cross_right = has_right & (lax.rem(col, 2) == 1)
    near_left = has_left & (lax.rem(col, 2) == 1)
    near_right = has_right & (lax.rem(col, 2) == 0)

    bar = pltpu.get_barrier_semaphore()

    def greet(t, r, c):
        pl.semaphore_signal(bar, inc=1, device_id=(t, r, c), device_id_type=MESH)

    for o in range(1, nrow):
        greet(tm, lax.rem(row + o, nrow), col)
    greet(tm_prev, row, col)

    @pl.when(cross_right)
    def _():
        greet(tm, row, col + 1)
        greet(tm_prev, row, col + 1)
        greet(tm_next, row, col + 1)

    @pl.when(near_left)
    def _():
        greet(tm, row, col - 1)
        greet(tm_prev, row, col - 1)

    @pl.when(near_right)
    def _():
        greet(tm, row, col + 1)
        greet(tm_prev, row, col + 1)

    own_key = local(keys.at[0], KV, loc_sem.at[0])
    edge_l = local(feat.at[:, :, pl.ds(0, 16), :], FE.at[0], loc_sem.at[1])
    edge_r = local(feat.at[:, :, pl.ds(X - 16, 16), :], FE.at[1], loc_sem.at[2])
    own_feat = local(feat.at[row], F.at[row], loc_sem.at[3])
    weights = [local(mw, MW, loc_sem.at[4]), local(fw, FW, loc_sem.at[5])]
    for i in range(3):
        for o in range(2):
            half = pl.ds(128 * o, 128)
            weights.append(local(jw.at[i, :, pl.ds(0, C), :], WM.at[i + o, :, :, half], w_sem.at[0, i, o]))
            weights.append(local(jw.at[i, :, pl.ds(C, C), :], WF.at[i + o, :, :, half], w_sem.at[1, i, o]))
            weights.append(local(dw.at[i], W2.at[i + o, :, half], w_sem.at[2, i, o]))

    own_key.wait()
    ri = lax.broadcasted_iota(jnp.int32, (X, X), 0)
    ci = lax.broadcasted_iota(jnp.int32, (X, X), 1)
    turn = (ri + ci == X - 1).astype(F32).astype(BF)
    for yy in range(R):
        KK[1, yy] = dot(turn, KV[yy]).astype(BF)

    edge_l.wait()
    edge_r.wait()
    for side in range(2):
        kv = KK[1, :, :16, :].astype(F32)[:, :8, :] if side else KK[1, :, X - 16 :, :].astype(F32)[:, 8:, :]
        ES_K[side] = kv.reshape(R * 8, C).astype(BF)
        for f in range(NF):
            fv = FE[side, f].astype(F32)[:, 8 * side : 8 * side + 8, :]
            ES_F[side, f] = fv.reshape(R * 8, C).astype(BF)

    one = lambda flag, n: n * flag.astype(jnp.int32)
    pl.semaphore_wait(bar, nrow + one(near_left, 2) + one(near_right, 2) + one(cross_left, 3))

    @pl.when(cross_left)
    def _():
        for t in (tm, tm_prev):
            pl.semaphore_signal(ready, inc=1, device_id=(t, row, col - 1), device_id_type=MESH)

    def remote(src, dst, s, r, dev):
        return pltpu.make_async_remote_copy(
            src_ref=src, dst_ref=dst, send_sem=s, recv_sem=r, device_id=dev, device_id_type=MESH
        )

    def edge_copies(side):
        other = 1 - side
        c = col + 2 * side - 1
        return [
            remote(ES_K.at[side], EK[other].at[0], esend.at[side, 0], erecv.at[other, 0], (tm_next, row, c)),
            remote(ES_K.at[side], EK[other].at[1], esend.at[side, 1], erecv.at[other, 1], (tm, row, c)),
            remote(ES_F.at[side], EF.at[other], esend.at[side, 2], erecv.at[other, 2], (tm, row, c)),
        ]

    def edge_waits(side):
        c = col + 2 * side - 1
        return [
            remote(ES_K.at[side], EK[side].at[0], esend.at[side, 0], erecv.at[side, 0], (tm_next, row, c)),
            remote(ES_K.at[side], EK[side].at[1], esend.at[side, 1], erecv.at[side, 1], (tm, row, c)),
            remote(ES_F.at[side], EF.at[side], esend.at[side, 2], erecv.at[side, 2], (tm, row, c)),
        ]

    def start_edges(side):
        to_next, *others = edge_copies(side)
        for cp in others:
            cp.start()

        @pl.when(has_next)
        def _():
            to_next.start()

    for side, go in ((0, has_left), (1, near_right)):

        @pl.when(go)
        def _(side=side):
            start_edges(side)

    key_copy = remote(KK.at[1], KK.at[0], ksend, krecv, (tm_next, row, col))

    @pl.when(has_next)
    def _():
        key_copy.start()

    feat_copies = []
    for o in (2, 1, 3):
        there = lax.rem(row + o, nrow)
        cp = remote(feat.at[there], F.at[row], fsend.at[o - 1], frecv.at[o - 1], (tm, there, col))
        cp.start()
        feat_copies.append(cp)

    for w in weights:
        w.wait()
    q = lax.broadcasted_iota(jnp.int32, (256, 81), 0)
    d = lax.broadcasted_iota(jnp.int32, (256, 81), 1)
    t = q & 15
    pick = (d == 9 * (q >> 4) + 15 - t) & (t >= 7) & (q < 144)
    WR[...] = dot(pick.astype(F32).astype(BF), MW[...]).astype(BF)

    zero = jnp.zeros((3, 128, 128), BF)
    for w in (WM, WF):
        w[0, :, :, 128:256] = zero
        w[3, :, :, 0:128] = zero
    W2[0, :, 128:256] = zero.reshape(384, 128)
    W2[3, :, 0:128] = zero.reshape(384, 128)
    W4[...] = jnp.zeros_like(W4)
    for j in range(3):
        for i in range(3):
            W4[8 * j + 2 * i : 8 * j + 2 * i + 2, :] = FW[:, 384 * i + 128 * j : 384 * i + 128 * j + 128].astype(F32)
    for i in (0, H + 1):
        JF[i] = jnp.zeros((D, 384), BF)
        JM[i] = jnp.zeros((D, 384), BF)
        RS[i] = jnp.zeros((8, X), F32)
    for i in (0, 1, H + 2, H + 3):
        H3[i] = jnp.zeros((D, 384), BF)
    KR[:, 0:8, :] = jnp.zeros((H, 8, C), F32)
    KR[:, E - 16 :, :] = jnp.zeros((H, 16, C), F32)
    MF[:, 0:8, :] = jnp.zeros((H, 8, C), F32)
    MF[:, D + 8 :, :] = jnp.zeros((H, 8, C), F32)

    dd = lax.broadcasted_iota(jnp.int32, (D, C), 0)
    inside = (has_left | (dd >= 8)) & (has_right | (dd < X + 8))

    slots = [
        jnp.where(kidx[lax.rem(row + o, nrow)] == tm, 1, 0) for o in range(nrow)
    ]

    def border_copies(side):
        return [
            remote(
                SH.at[side, o - 1],
                RH.at[row, side],
                hsend.at[side, o - 1],
                hrecv.at[side, o - 1],
                (tm, lax.rem(row + o, nrow), col),
            )
            for o in (2, 1, 3)
        ]

    def fill_border(dst, o, side):
        dst[0:32, :] = EK[side][slots[o]]
        dst[32:64, :] = EF[side, lax.rem(row + o, nrow)]

    def pass_border(side):
        from_prev, *others = edge_waits(side)
        for cp in others:
            cp.wait_recv()

        @pl.when(has_prev)
        def _():
            from_prev.wait_recv()

        for o, cp in zip((2, 1, 3), border_copies(side)):
            fill_border(SH.at[side, o - 1], o, side)
            cp.start()
        fill_border(RH.at[row, side], 0, side)

    @pl.when(near_left)
    def _():
        pass_border(0)

    @pl.when(near_right)
    def _():
        pass_border(1)


    @pl.when(has_next)
    def _():
        key_copy.wait_send()

    @pl.when(has_prev)
    def _():
        key_copy.wait_recv()

    msg_copies = []
    for k in range(NCH):
        if k == 1:

            @pl.when(cross_left)
            def _():
                pass_border(0)

        if k == 2:

            @pl.when(cross_right)
            def _():
                pl.semaphore_wait(ready, 2)
                start_edges(1)

        if k == 3:

            @pl.when(cross_right)
            def _():
                pass_border(1)

        part = slice(X - (k + 1) * CH, X - k * CH)
        ds = pl.ds(X - (k + 1) * CH, CH)
        copies = []
        for o in (2, 1, 3):
            there = lax.rem(row + o, nrow)
            SB[o - 1, :, part, :] = KK[slots[o], :, part, :]
            cp = remote(
                SB.at[o - 1, :, ds, :], RB.at[row, :, ds, :], msend.at[k, o - 1], mrecv.at[k, o - 1], (tm, there, col)
            )
            cp.start()
            copies.append(cp)
        msg_copies.append(copies)
    RB[row] = KK[slots[0]]

    own_feat.wait()
    for cp in feat_copies:
        cp.wait_recv()
    edge = jnp.zeros((8, C), F32)

    def arrange(rs, carry):
        for yy in range(R):
            y = R * rs + yy
            fr = jnp.concatenate([edge, F[rs, yy].astype(F32), edge], axis=0)
            FQ[y] = fr
            for j in range(3):
                sh = fr if j == 1 else pltpu.roll(fr, (1 - j) % D, 0)
                JF[y + 1, :, 128 * j : 128 * j + 128] = sh.astype(BF)
        return carry

    lax.fori_loop(0, NF, arrange, 0)

    def pairs(src, first, gap):
        return jnp.concatenate(
            [
                jnp.concatenate([src[first + t * (3 - gap)] for t in range(4)], axis=1),
                jnp.concatenate([src[first + gap + t * (3 - gap)] for t in range(4)], axis=1),
            ],
            axis=0,
        )

    def joint_frames(p, carry):
        HF[p] = dot(pairs(JF, 4 * p, 2), WF[...].reshape(1536, 256))
        return carry

    lax.fori_loop(0, H // 4, joint_frames, 0)

    scale = 1.0 / math.sqrt(C)
    lane = lax.broadcasted_iota(jnp.int32, (8, 128), 1)

    def correlate(p, carry):
        parts = [[], []]
        for h in range(2):
            d0 = pl.multiple_of(16 * p + 8 * h, 8)
            e0 = pl.multiple_of(136 - 16 * p - 8 * h, 8)
            qs = FQ[:, pl.ds(d0, 8), :].reshape(H * 8, C).astype(BF)
            ks = KR[:, pl.ds(e0, 16), :].reshape(H * 16, C).astype(BF)
            sc = (dot_t(qs, ks) * scale).reshape(H, 8, 256)
            for y in range(H):
                turn = (64 - 16 * y) % 256
                by = turn % 128
                lo = pltpu.roll(sc[y, :, :128], by, 1, stride=1, stride_axis=0)
                hi = pltpu.roll(sc[y, :, 128:], by, 1, stride=1, stride_axis=0)
                if turn >= 128:
                    lo, hi = hi, lo
                low = jnp.where(lane < by, hi, lo) if by else lo
                high = jnp.where(lane < by, lo, hi) if by else hi
                if y < 4:
                    low = jnp.where(lane >= 16 * (4 - y), low, 0.0)
                if y > 11:
                    high = jnp.zeros_like(high)
                if y > 12:
                    low = jnp.where(lane < 16 * (20 - y), low, 0.0)
                parts[h].append(jnp.concatenate([low, high], axis=1))
        c0 = pl.multiple_of(16 * p, 16)
        for y in range(H):
            CB[y, pl.ds(c0, 16), :] = jnp.concatenate([parts[0][y], parts[1][y]], axis=0).astype(BF)
        return carry

    def motion(corr, keep):
        n = corr.shape[1]
        m = dot(corr.reshape(H * n, 256), WR[...]).reshape(H, n, C)
        return jnp.where(keep[None], jnp.maximum(m, 0.0), 0.0)

    def shift(d0, d1):
        def shifts(y, carry):
            for j in range(3):
                JM[y + 1, d0:d1, 128 * j : 128 * j + 128] = MF[y, 7 + j + d0 : 7 + j + d1, :].astype(BF)
            return carry

        lax.fori_loop(0, H, shifts, 0, unroll=True)

    def amend(rs, carry):
        left = jnp.where(has_left, RH[rs, 0].astype(F32), 0.0)
        right = jnp.where(has_right, RH[rs, 1].astype(F32), 0.0)
        for yy in range(R):
            y = R * rs + yy
            b = 8 * yy
            KR[y, 140:148, :] = left[b : b + 8]
            KR[y, 4:12, :] = right[b : b + 8]
            lf, rf = left[32 + b : 40 + b], right[32 + b : 40 + b]
            FQ[y, 0:8, :] = lf
            FQ[y, D - 8 : D, :] = rf
            ends = (
                jnp.concatenate([lf, F[rs, yy, 0:16, :].astype(F32)], axis=0),
                jnp.concatenate([F[rs, yy, X - 16 :, :].astype(F32), rf], axis=0),
            )
            for side, at in ((0, 0), (1, D - 16)):
                for j in range(3):
                    sh = ends[side] if j == 1 else pltpu.roll(ends[side], (1 - j) % 24, 0)
                    JF[y + 1, at : at + 16, 128 * j : 128 * j + 128] = sh[8 * side : 8 * side + 16].astype(BF)
        return carry

    done = 1
    shifted = 32
    for k in range(NCH):
        if k == NCH - 1:
            for side, has in ((0, has_left), (1, has_right)):

                @pl.when(has)
                def _(side=side):
                    for cp in border_copies(side):
                        cp.wait_recv()

            lax.fori_loop(0, NF, amend, 0)

            spots = [(p, u, at) for p in range(H // 4) for u in range(2) for at in (0, D - 16)]
            lhs = jnp.concatenate(
                [
                    jnp.concatenate([JF[4 * p + 2 * u + t, at : at + 16, :] for t in range(4)], axis=1)
                    for p, u, at in spots
                ],
                axis=0,
            )
            hf = dot(lhs, WF[...].reshape(1536, 256))
            for i, (p, u, at) in enumerate(spots):
                HF[p, D * u + at : D * u + at + 16, :] = hf[16 * i : 16 * i + 16]

            correlate(0, 0)
            MF[:, 8:24, :] = motion(CB[:, 0:16, :], inside[0:16])
            shift(0, 32)

        for cp in msg_copies[k]:
            cp.wait_recv()
        s0 = X - (k + 1) * CH

        def place(rs, carry, s0=s0):
            y0 = R * rs
            for yy in range(R):
                KR[y0 + yy, 12 + s0 : 12 + s0 + CH, :] = RB[rs, yy, s0 : s0 + CH, :].astype(F32)
            return carry

        lax.fori_loop(0, NF, place, 0, unroll=True)
        upto = D // 16 if k == NCH - 1 else ((k + 1) * CH - 12) // 16 + 1
        lax.fori_loop(done, upto, correlate, 0, unroll=k == NCH - 1)
        d0, d1 = 16 * done, 16 * upto
        MF[:, d0 + 8 : d1 + 8, :] = motion(CB[:, d0:d1, :], inside[d0:d1])
        done = upto
        d1 = D if k == NCH - 1 else d1 - 16
        if d1 > shifted:
            shift(shifted, d1)
            shifted = d1

    def joint(p, carry):
        h = dot(pairs(JM, 4 * p, 2), WM[...].reshape(1536, 256)) + HF[p]
        for u in range(2):
            for o in range(2):
                ho = h[D * u : D * u + D, 128 * o : 128 * o + 128]
                ho = jnp.where(inside, jnp.maximum(ho, 0.0), 0.0)
                for j in range(3):
                    sh = ho if j == 1 else pltpu.roll(ho, (2 - 2 * j) % D, 0)
                    H3[4 * p + 2 * u + o + 2, :, 128 * j : 128 * j + 128] = sh.astype(BF)
        return carry

    lax.fori_loop(0, H // 4, joint, 0, unroll=True)

    def dilated(p, carry):
        h = dot(pairs(H3, 4 * p, 1), W2[...].reshape(1536, 256))
        for yy in range(R):
            u, o = yy % 2, yy // 2
            ho = h[D * u : D * u + D, 128 * o : 128 * o + 128]
            HB[R * p + yy] = jnp.where(inside, jnp.maximum(ho, 0.0), 0.0).astype(BF)
        return carry

    def taps(p, carry):
        res = dot_t(W4[...].astype(BF), HB[pl.ds(R * p, R)].reshape(R * D, C))
        for yy in range(R):
            RS[R * p + yy + 1] = sum(
                res[8 * j : 8 * j + 8, D * yy + 7 + j : D * yy + 7 + j + X] for j in range(3)
            )
        return carry

    def head(rr, carry):
        for yy in range(R):
            y = R * rr + yy
            res = RS[y, 0:2, :] + RS[y + 1, 2:4, :] + RS[y + 2, 4:6, :]
            OS[rr, :, yy : yy + 1, :] = res.reshape(2, 1, X)
        return carry

    own_out = pltpu.make_async_copy(OS.at[row], out.at[row], loc_sem.at[6])

    def send_tile(rr):
        o = lax.rem(rr - row + nrow, nrow)

        @pl.when(row != rr)
        def _():
            remote(OS.at[rr], out.at[row], osend.at[o - 1], orecv.at[o - 1], (tm, rr, col)).start()

        @pl.when(row == rr)
        def _():
            own_out.start()

    out_copies = [
        remote(
            OS.at[lax.rem(row + o, nrow)],
            out.at[row],
            osend.at[o - 1],
            orecv.at[o - 1],
            (tm, lax.rem(row + o, nrow), col),
        )
        for o in range(1, nrow)
    ]
    for parts, tiles in PLAN:
        for p in parts:
            dilated(p, 0)
        for p in parts:
            taps(p, 0)
        for p in tiles:
            head(p, 0)
        for p in tiles:
            send_tile(p)
    own_out.wait()
    for cp in out_copies:
        cp.wait_recv()

    for cp in feat_copies + sum(msg_copies, []) + out_copies:
        cp.wait_send()
    for side, has in ((0, has_left), (1, has_right)):

        @pl.when(has)
        def _(side=side):
            to_next, *others = edge_copies(side)
            for cp in others + border_copies(side):
                cp.wait_send()

            @pl.when(has_next)
            def _():
                to_next.wait_send()


def solution(mesh):
    ntm, ncol = mesh.shape["tm"], mesh.shape["col"]

    def step(feat, keys, kidx, mw, jw, dw, fw):
        anyspec = pl.BlockSpec(memory_space=pltpu.HBM)
        dma = pltpu.SemaphoreType.DMA
        return pl.pallas_call(
            functools.partial(kernel, ntm, ncol),
            out_shape=jax.ShapeDtypeStruct((NF, 2, R, X), F32),
            in_specs=[
                pl.BlockSpec(memory_space=pltpu.SMEM),
                anyspec,
                anyspec,
                anyspec,
                anyspec,
                anyspec,
                anyspec,
            ],
            out_specs=anyspec,
            scratch_shapes=[
                pltpu.VMEM((NF, R, X, C), BF),
                pltpu.VMEM((2, R, X, C), BF),
                pltpu.VMEM((R, X, C), BF),
                pltpu.VMEM((2, NF, R, 16, C), BF),
                pltpu.VMEM((2, R * 8, C), BF),
                pltpu.VMEM((2, NF, R * 8, C), BF),
                pltpu.VMEM((2, R * 8, C), BF),
                pltpu.VMEM((2, R * 8, C), BF),
                pltpu.VMEM((2, NF, R * 8, C), BF),
                pltpu.VMEM((3, R, X, C), BF),
                pltpu.VMEM((NF, R, X, C), BF),
                pltpu.VMEM((2, 3, 64, C), BF),
                pltpu.VMEM((NF, 2, 64, C), BF),
                pltpu.VMEM((81, C), BF),
                pltpu.VMEM((2, 9 * C), BF),
                pltpu.VMEM((H, D, C), F32),
                pltpu.VMEM((H, E, C), F32),
                pltpu.VMEM((H, D, 256), BF),
                pltpu.VMEM((256, C), BF),
                pltpu.VMEM((H, D + 16, C), F32),
                pltpu.VMEM((H + 2, D, 384), BF),
                pltpu.VMEM((H + 2, D, 384), BF),
                pltpu.VMEM((4, 3, C, 256), BF),
                pltpu.VMEM((4, 3, C, 256), BF),
                pltpu.VMEM((H // 4, 2 * D, 256), F32),
                pltpu.VMEM((H + 4, D, 384), BF),
                pltpu.VMEM((4, 384, 256), BF),
                pltpu.VMEM((24, C), F32),
                pltpu.VMEM((H, D, C), BF),
                pltpu.VMEM((H + 2, 8, X), F32),
                pltpu.VMEM((NF, 2, R, X), F32),
                dma((7,)),
                dma((3, 3, 2)),
                dma,
                dma,
                dma((2, 3)),
                dma((2, 3)),
                dma((3,)),
                dma((3,)),
                dma((NCH, 3)),
                dma((NCH, 3)),
                dma((3,)),
                dma((3,)),
                pltpu.SemaphoreType.REGULAR,
                dma((2, 3)),
                dma((2, 3)),
            ],
            compiler_params=pltpu.CompilerParams(
                collective_id=0, has_side_effects=True, vmem_limit_bytes=60 * 1024 * 1024
            ),
        )(
            kidx.reshape(NF),
            feat,
            keys,
            mw,
            jw,
            dw.reshape(3, 384, 128),
            fw.reshape(2, 1152),
        )

    in_specs = (
        P("tm", "row", "col", None),
        P("tm", "row", "col", None),
        P("tm", None),
        P(),
        P(),
        P(),
        P(),
    )
    return jax.shard_map(
        step, mesh=mesh, in_specs=in_specs, out_specs=P("tm", None, "row", "col"), check_vma=False
    )
```
